128 devices in a mesh: seq: 16 (over x, y_lo, core), fsdp: 8 (over z, y_hi).
Axes of the slice: x: 4, y: 4 (y_hi: 2, y_lo: 2; y = y_hi * 2 + y_lo), z: 4, core: 2. Of those that a mesh axis runs over, the one named last changes fastest.
Arguments:
- clip_tokens: bfloat16 [16, 256, 3584], P('seq'), may hold values from -6 to 6
- out_cotangent: bfloat16 [16, 256, 3584], P(None, 'seq'), may hold values from -6 to 6
- proj_weight: bfloat16 [2, 3584, 6144], P(None, 'seq', 'fsdp'), may hold values from -0.09375 to 0.09375
- out_weight: bfloat16 [2, 2048, 3584], P(None, 'fsdp', 'seq'), may hold values from -0.125 to 0.125
- norm_gain: float32 [2, 3584], replicated, may hold values from 0.1 to 1.9
- branch_gate: float32 [2, 3584], replicated, may hold values from 0.1 to 1.9
- qk_gain: float32 [2, 2, 128], replicated, may hold values from 0.1 to 1.9
Outputs:
- mixed_out: bfloat16 [16, 256, 3584], P(None, 'seq')
- grad_clip: bfloat16 [16, 256, 3584], P('seq')
- grad_proj: bfloat16 [2, 3584, 6144], P(None, 'seq', 'fsdp')
- grad_outw: bfloat16 [2, 2048, 3584], P(None, 'fsdp', 'seq')
The draws below stay inside these ranges and needn't reach their ends.
All inputs are finite; a program needn't handle non-finite values.
Results may differ from the reference program's by a relative error of at most 0.035.
Values may be sent and summed in bfloat16 or wider, within the bound.
A program may use at most 128 MiB of HBM per device.

```python
from functools import partial
import jax
import jax.numpy as jnp
from jax import lax

D = 3584
HD = 128
H_DEV = 2
P_DEV = 16
HEADS = 16
FRAMES = 16
S = 256
N_SEQ = 16
N_FSDP = 8


def levels(rng, dims, split, low, largest):
    factor_of = 1.0
    for position, parts in split:
        heights = jax.random.uniform(jax.random.fold_in(jax.random.fold_in(rng, 6), position), (parts,), jnp.float32, low / len(split), largest / len(split))
        factor_of = factor_of * jnp.repeat(jnp.exp(heights), dims[position] // parts).reshape((-1,) + (1,) * (len(dims) - 1 - position))
    return factor_of


def centred(stream_key, extent, spread, bound, cuts=(), held_as=jnp.bfloat16):
    drawn = spread * jax.random.normal(stream_key, extent, jnp.float32)
    if cuts:
        drawn = drawn * levels(stream_key, extent, cuts, -0.22, 0.18)
    return jnp.clip(drawn, -bound, bound).astype(held_as)


def setup_inputs(seed: int = 0) -> dict:
    streams_of = jax.random.split(jax.random.key(seed), 8)
    return {
        "clip_tokens": centred(streams_of[0], (FRAMES, S, D), 1.0, 6.0, ((0, 16),)),
        "out_cotangent": centred(streams_of[1], (FRAMES, S, D), 1.0, 6.0, ((1, 16),)),
        "proj_weight": centred(streams_of[2], (2, D, HEADS * 3 * HD), D ** -0.5, 0.09375, ((1, 16), (2, 8))),
        "out_weight": centred(streams_of[3], (2, HEADS * HD, D), (HEADS * HD) ** -0.5, 0.125, ((1, 8), (2, 16))),
        "norm_gain": jnp.clip(1.0 + 0.18 * jax.random.normal(streams_of[4], (2, D), jnp.float32), 0.1, 1.9),
        "branch_gate": jnp.clip(1.0 + 0.18 * jax.random.normal(streams_of[5], (2, D), jnp.float32), 0.1, 1.9),
        "qk_gain": jnp.clip(1.0 + 0.18 * jax.random.normal(streams_of[6], (2, 2, HD), jnp.float32), 0.1, 1.9),
    }


EPS = 1e-06

def shapes(temporal):
    if temporal:
        return ('lghe,mghe->ghlm', 'ghlm,mghe->lghe')
    return ('glhe,gmhe->ghlm', 'ghlm,gmhe->glhe')

def unit_norm(values_in, gain):
    return values_in * lax.rsqrt(lax.optimization_barrier(jnp.mean(values_in * values_in, -1, keepdims=True)) + EPS) * gain

def attend(projected, qk_gain, temporal):
    score_form, mix_form = shapes(temporal)
    head_width = projected.shape[-1]
    query_rows = unit_norm(projected[..., 0, :], qk_gain[0]).astype(jnp.bfloat16)
    key_rows = unit_norm(projected[..., 1, :], qk_gain[1]).astype(jnp.bfloat16)
    value_rows = projected[..., 2, :].astype(jnp.bfloat16)
    scores = jnp.einsum(score_form, query_rows.astype(jnp.float32), key_rows.astype(jnp.float32)) * head_width ** (-0.5)
    probs = jax.nn.softmax(scores, axis=-1).astype(jnp.bfloat16)
    return jnp.einsum(mix_form, probs.astype(jnp.float32), value_rows.astype(jnp.float32)).astype(jnp.bfloat16)

def grouped(left, right, span):
    summed = jnp.zeros(left.shape[:-1] + (right.shape[1],), jnp.float32)
    for member in range(N_FSDP):
        portion = jnp.dot(left[..., member * span:(member + 1) * span], right[member * span:(member + 1) * span], preferred_element_type=jnp.float32)
        summed = summed + lax.optimization_barrier(portion.astype(jnp.bfloat16)).astype(jnp.float32)
    return summed

def pieces(inputs, gain, qk_gain, proj_weight, temporal):
    widened = inputs.astype(jnp.float32)
    inverse = lax.rsqrt(lax.optimization_barrier(jnp.mean(widened * widened, -1, keepdims=True)) + EPS)
    normed = (widened * inverse * gain).astype(jnp.bfloat16)
    projected = jnp.dot(normed, proj_weight, preferred_element_type=jnp.float32)
    projected = projected.reshape(inputs.shape[0], inputs.shape[1], HEADS, 3, HD)
    attended = attend(projected, qk_gain, temporal).reshape(inputs.shape[0], inputs.shape[1], HEADS * HD)
    return (normed, inverse, projected, attended)

def advance(inputs, gain, gate, qk_gain, proj_weight, out_weight, temporal):
    attended = pieces(inputs, gain, qk_gain, proj_weight, temporal)[3]
    summed = grouped(attended, out_weight, H_DEV * HD)
    return (inputs.astype(jnp.float32) + gate * summed).astype(jnp.bfloat16)

def token_sets(array, temporal):
    if temporal:
        array = jnp.swapaxes(array.reshape(array.shape[0], N_SEQ, P_DEV, array.shape[-1]), 0, 1)
    return array.reshape(N_SEQ, -1, array.shape[-1])

def shard_sum(left, right, temporal):
    left_sets = token_sets(left, temporal)
    right_sets = token_sets(right, temporal)

    def accumulate(summed, pair):
        portion = lax.dot_general(pair[0], pair[1], (((0,), (0,)), ((), ())), preferred_element_type=jnp.float32)
        return (summed + lax.optimization_barrier(portion.astype(jnp.bfloat16)).astype(jnp.float32), None)
    start_value = jnp.zeros((left.shape[-1], right.shape[-1]), jnp.float32)
    return lax.scan(accumulate, start_value, (left_sets, right_sets))[0]

def retreat(inputs, cotangent, gain, gate, qk_gain, proj_weight, out_weight, temporal):
    normed, inverse, projected, attended = pieces(inputs, gain, qk_gain, proj_weight, temporal)
    count_a, count_b = (inputs.shape[0], inputs.shape[1])
    scaled = (cotangent.astype(jnp.float32) * gate).astype(jnp.bfloat16)
    grad_wout = shard_sum(attended, scaled, temporal)
    grad_att = lax.dot_general(scaled, out_weight, (((2,), (1,)), ((), ())), preferred_element_type=jnp.float32)
    grad_att = grad_att.astype(jnp.bfloat16).reshape(count_a, count_b, HEADS, HD)
    pullback = jax.vjp(partial(attend, qk_gain=qk_gain, temporal=temporal), projected)[1]
    grad_projected = pullback(grad_att)[0].astype(jnp.bfloat16).reshape(count_a, count_b, HEADS * 3 * HD)
    grad_wproj = shard_sum(normed, grad_projected, temporal)
    grad_normed = grouped(grad_projected, proj_weight.T, H_DEV * 3 * HD)
    widened = inputs.astype(jnp.float32)
    weighted = grad_normed * gain
    grad_input = inverse * weighted - widened * inverse ** 3 * lax.optimization_barrier(jnp.mean(widened * weighted, -1, keepdims=True))
    return ((cotangent.astype(jnp.float32) + grad_input).astype(jnp.bfloat16), grad_wproj, grad_wout)

def reference(clip_tokens, out_cotangent, proj_weight, out_weight, norm_gain, branch_gate, qk_gain):
    middle = advance(clip_tokens, norm_gain[0], branch_gate[0], qk_gain[0], proj_weight[0], out_weight[0], False)
    mixed_out = advance(middle, norm_gain[1], branch_gate[1], qk_gain[1], proj_weight[1], out_weight[1], True)
    grad_middle, proj_late, outw_late = retreat(middle, out_cotangent, norm_gain[1], branch_gate[1], qk_gain[1], proj_weight[1], out_weight[1], True)
    grad_clip, proj_early, outw_early = retreat(clip_tokens, grad_middle, norm_gain[0], branch_gate[0], qk_gain[0], proj_weight[0], out_weight[0], False)
    grad_proj = jnp.stack([proj_early, proj_late]).astype(jnp.bfloat16)
    grad_outw = jnp.stack([outw_early, outw_late]).astype(jnp.bfloat16)
    return (mixed_out, grad_clip, grad_proj, grad_outw)
```

```python
import functools

import jax
import jax.numpy as jnp
from jax import lax
from jax.experimental import pallas as pl
from jax.experimental.pallas import tpu as pltpu
from jax.sharding import PartitionSpec as P

EPS = 1e-06
MESH = pl.DeviceIdType.MESH
D = 3584
HD = 128
T = 256
NF = 8
OWN = T // NF
SH = 224
WC = 1024
PC = 768
TILE = 512
NT = D // TILE
F32 = jnp.float32
BF16 = jnp.bfloat16
VMEM_LIMIT = 60 * 1024 * 1024


def tile_at(i, size=TILE):
    return pl.ds(pl.multiple_of(i * size, size), size)


def dot(a, b, contract=((1,), (0,))):
    return lax.dot_general(a, b, (contract, ((), ())), preferred_element_type=F32)


def head_forward(proj_ref, qkg, head, temporal):
    base = head * 3 * HD
    q_raw = proj_ref[:, base : base + HD]
    k_raw = proj_ref[:, base + HD : base + 2 * HD]
    q_inv = lax.rsqrt(jnp.mean(q_raw * q_raw, -1, keepdims=True) + EPS)
    k_inv = lax.rsqrt(jnp.mean(k_raw * k_raw, -1, keepdims=True) + EPS)
    q = (q_raw * q_inv * qkg[0:1, :]).astype(BF16)
    k = (k_raw * k_inv * qkg[1:2, :]).astype(BF16)
    v = proj_ref[:, base + 2 * HD : base + 3 * HD].astype(BF16)
    scores = dot(q, k, ((1,), (1,))) * HD**-0.5
    if temporal:
        rows = lax.broadcasted_iota(jnp.int32, (T, T), 0)
        cols = lax.broadcasted_iota(jnp.int32, (T, T), 1)
        scores = jnp.where((rows & 15) == (cols & 15), scores, -1e30)
    top = jnp.max(scores, -1, keepdims=True)
    grown = jnp.exp(scores - top)
    probs = grown / jnp.sum(grown, -1, keepdims=True)
    return q_raw, k_raw, q_inv, k_inv, q, k, v, probs


def head_backward(proj_ref, qkg, head, temporal, d_att, dproj_ref):
    q_raw, k_raw, q_inv, k_inv, q, k, v, probs = head_forward(proj_ref, qkg, head, temporal)
    base = head * 3 * HD
    rounded = probs.astype(BF16)
    d_probs = dot(d_att, v, ((1,), (1,))).astype(BF16).astype(F32)
    d_v = dot(rounded, d_att, ((0,), (0,)))
    d_scores = probs * (d_probs - jnp.sum(probs * d_probs, -1, keepdims=True))
    d_scores = (d_scores * HD**-0.5).astype(BF16)
    d_q = dot(d_scores, k).astype(BF16).astype(F32) * qkg[0:1, :]
    d_k = dot(d_scores, q, ((0,), (0,))).astype(BF16).astype(F32) * qkg[1:2, :]
    d_q = q_inv * d_q - q_raw * (q_inv * q_inv * q_inv) * jnp.mean(q_raw * d_q, -1, keepdims=True)
    d_k = k_inv * d_k - k_raw * (k_inv * k_inv * k_inv) * jnp.mean(k_raw * d_k, -1, keepdims=True)
    dproj_ref[:, base : base + HD] = d_q.astype(BF16)
    dproj_ref[:, base + HD : base + 2 * HD] = d_k.astype(BF16)
    dproj_ref[:, base + 2 * HD : base + 3 * HD] = d_v.astype(BF16)


def block_forward(x_ref, w_ref, gain_ref, qkg, normed_ref, proj_ref, att_ref, part_ref, temporal):
    def square(i, total):
        x = x_ref[:, tile_at(i)].astype(F32)
        return total + jnp.sum(x * x, -1, keepdims=True)

    total = lax.fori_loop(0, NT, square, jnp.zeros((T, 1), F32))
    inverse = lax.rsqrt(total / D + EPS)
    proj_ref[...] = jnp.zeros_like(proj_ref)

    @pl.loop(0, NT)
    def _(i):
        at = tile_at(i)
        normed = (x_ref[:, at].astype(F32) * inverse * gain_ref[:, at]).astype(BF16)
        normed_ref[:, at] = normed
        proj_ref[...] += dot(normed, w_ref[at, :PC])

    for head in range(2):
        parts = head_forward(proj_ref, qkg, head, temporal)
        att_ref[:, head * HD : (head + 1) * HD] = dot(parts[7].astype(BF16), parts[6]).astype(BF16)
    att = att_ref[...]

    @pl.loop(0, NT)
    def _(i):
        at = tile_at(i)
        part_ref[:, at] = dot(att, w_ref[at, PC:], ((1,), (1,))).astype(BF16)


def block_backward(
    dy_ref, w_ref, gate_ref, qkg, normed_ref, proj_ref, att_ref, dpart_ref, g_ref, datt_ref, dproj_ref, temporal
):
    datt_ref[...] = jnp.zeros_like(datt_ref)

    @pl.loop(0, NT)
    def _(i):
        at = tile_at(i)
        scaled = (dy_ref[:, at].astype(F32) * gate_ref[:, at]).astype(BF16)
        datt_ref[...] += dot(scaled, w_ref[at, PC:])

    for head in range(2):
        d_att = datt_ref[:, head * HD : (head + 1) * HD].astype(BF16)
        head_backward(proj_ref, qkg, head, temporal, d_att, dproj_ref)
    dproj = dproj_ref[...]
    att = att_ref[...]

    @pl.loop(0, NT)
    def _(i):
        at = tile_at(i)
        dpart_ref[:, at] = dot(dproj, w_ref[at, :PC], ((1,), (1,))).astype(BF16)
        g_ref[at, :PC] = dot(normed_ref[:, at], dproj, ((0,), (0,))).astype(BF16)
        scaled = (dy_ref[:, at].astype(F32) * gate_ref[:, at]).astype(BF16)
        g_ref[at, PC:] = dot(scaled, att, ((0,), (0,))).astype(BF16)


def spatial_forward(x_ref, w_ref, gain_ref, qkg_ref, normed_ref, proj_ref, att_ref, part_ref):
    block_forward(x_ref, w_ref, gain_ref, qkg_ref[...], normed_ref, proj_ref, att_ref, part_ref, False)


def spatial_backward(
    dy_ref, w_ref, gate_ref, qkg_ref, normed_ref, proj_ref, att_ref, dpart_ref, g_ref, datt_ref, dproj_ref
):
    block_backward(
        dy_ref, w_ref, gate_ref, qkg_ref[...], normed_ref, proj_ref, att_ref, dpart_ref, g_ref, datt_ref, dproj_ref, False
    )


def temporal_both(
    x_ref, dy_ref, w_ref, gain_ref, gate_ref, qkg_ref, part_ref, dpart_ref, g_ref, normed_ref, proj_ref, att_ref, datt_ref, dproj_ref
):
    qkg = qkg_ref[...]
    block_forward(x_ref, w_ref, gain_ref, qkg, normed_ref, proj_ref, att_ref, part_ref, True)
    block_backward(
        dy_ref, w_ref, gate_ref, qkg, normed_ref, proj_ref, att_ref, dpart_ref, g_ref, datt_ref, dproj_ref, True
    )


def place():
    return lax.axis_index("seq"), lax.axis_index("fsdp")


def remote(src, dst, send, recv, device):
    return pltpu.make_async_remote_copy(
        src_ref=src, dst_ref=dst, send_sem=send, recv_sem=recv, device_id=device, device_id_type=MESH
    )


def fsdp_peer(k):
    s, f = place()
    return (s, lax.rem(f + k, NF))


def chip_peer(k):
    s, f = place()
    return (2 * lax.rem(s // 2 + k, 8) + lax.rem(s, 2), f)


def sibling():
    s, f = place()
    return (s + 1 - 2 * lax.rem(s, 2), f)


def swap_peer(j):
    s, f = place()
    return (2 * f + j, s // 2)


def greet(with_fsdp, with_seq, with_swap):
    barrier = pltpu.get_barrier_semaphore()
    peers = []
    if with_fsdp:
        peers += [fsdp_peer(k) for k in range(1, 8)]
    if with_seq:
        peers += [chip_peer(k) for k in range(1, 8)] + [sibling()]
    count = len(peers)
    for peer in peers:
        pl.semaphore_signal(barrier, inc=1, device_id=peer, device_id_type=MESH)
    if with_swap:
        s, f = place()
        count = count + 2 - (s // 2 == f).astype(jnp.int32)
        for j in range(2):
            peer = swap_peer(j)

            @pl.when(jnp.logical_not(jnp.logical_and(s // 2 == f, lax.rem(s, 2) == j)))
            def _():
                pl.semaphore_signal(barrier, inc=1, device_id=peer, device_id_type=MESH)

    pl.semaphore_wait(barrier, count)


def rows_at(i, n):
    return pl.ds(pl.multiple_of(i * n, n), n)


class Gather:
    def __init__(self, proj_ref, outw_ref, w_ref, sems, local):
        self.proj_ref, self.outw_ref, self.w_ref, self.sems, self.local = proj_ref, outw_ref, w_ref, sems, local
        self.s, self.f = place()

    def start(self):
        rows = rows_at(self.s, SH)
        first = pltpu.make_async_copy(self.proj_ref, self.w_ref.at[rows, pl.ds(0, PC)], self.local.at[0])
        second = pltpu.make_async_copy(self.outw_ref, self.w_ref.at[rows, pl.ds(PC, WC - PC)], self.local.at[1])
        first.start()
        second.start()
        first.wait()
        second.wait()
        for k in range(1, 8):
            self.far(k).start()
        self.near(0).start()

    def far(self, k):
        rows = self.w_ref.at[rows_at(self.s, SH)]
        return remote(rows, rows, self.sems.at[0, k], self.sems.at[1, k], chip_peer(k))

    def near(self, k):
        rows = self.w_ref.at[rows_at(2 * lax.rem(self.s // 2 + 8 - k, 8) + lax.rem(self.s, 2), SH)]
        return remote(rows, rows, self.sems.at[2, k], self.sems.at[3, k], sibling())

    def relay(self):
        for k in range(1, 8):
            self.far(k).wait_recv()
            self.near(k).start()

    def finish(self):
        for k in range(1, 8):
            self.far(k).wait_send()
        for k in range(8):
            self.near(k).wait()


class Scatter:
    def __init__(self, part_ref, held_ref, sems):
        self.part_ref, self.held_ref, self.sems = part_ref, held_ref, sems

    def copy(self, k):
        _, f = place()
        src = self.part_ref.at[rows_at(lax.rem(f + k, NF), OWN)]
        return remote(src, self.held_ref.at[k - 1], self.sems.at[0, k], self.sems.at[1, k], fsdp_peer(k))

    def start(self):
        for k in range(1, 8):
            self.copy(k).start()

    def wait(self):
        for k in range(1, 8):
            self.copy(k).wait()

    def total(self, at):
        _, f = place()
        summed = self.part_ref[rows_at(f, OWN), at].astype(F32)
        for k in range(7):
            summed = summed + self.held_ref[k, :, at].astype(F32)
        return summed


class Spread:
    def __init__(self, ref, sems):
        self.ref, self.sems = ref, sems

    def copy(self, k):
        _, f = place()
        rows = self.ref.at[rows_at(f, OWN)]
        return remote(rows, rows, self.sems.at[0, k], self.sems.at[1, k], fsdp_peer(k))

    def start(self):
        for k in range(1, 8):
            self.copy(k).start()

    def wait(self):
        for k in range(1, 8):
            self.copy(k).wait()


def swap(src_ref, dst_ref, sems, local):
    s, f = place()
    for stage in range(2):
        for j in range(2):
            mine = jnp.logical_and(s // 2 == f, lax.rem(s, 2) == j)
            there = dst_ref.at[pl.ds(pl.multiple_of((s // 2) * OWN + lax.rem(s, 2) * 16, 16), 16)]
            src = src_ref.at[pl.ds(j * 16, 16)]
            here = dst_ref.at[pl.ds(pl.multiple_of(f * OWN + j * 16, 16), 16)]
            send = remote(src, there, sems.at[0, j], sems.at[1, lax.rem(s, 2)], swap_peer(j))
            arrival = remote(src, here, sems.at[0, j], sems.at[1, j], swap_peer(j))
            own = pltpu.make_async_copy(src, here, local)

            @pl.when(mine)
            def _():
                if stage == 0:
                    own.start()
                else:
                    own.wait()

            @pl.when(jnp.logical_not(mine))
            def _():
                if stage == 0:
                    send.start()
                else:
                    send.wait_send()
                    arrival.wait_recv()


class Reduce:
    def __init__(self, g_ref, sib_ref, out_ref, held_ref, sems):
        self.g_ref, self.sib_ref, self.out_ref, self.held_ref, self.sems = g_ref, sib_ref, out_ref, held_ref, sems
        self.s, self.f = place()
        self.chip, self.core = self.s // 2, lax.rem(self.s, 2)

    def near(self, k):
        rows = rows_at(2 * lax.rem(self.chip + k, 8) + 1 - self.core, SH)
        return remote(self.g_ref.at[rows], self.sib_ref.at[k], self.sems.at[0, k], self.sems.at[1, k], sibling())

    def far(self, k):
        return remote(
            self.out_ref.at[k - 1], self.held_ref.at[k - 1], self.sems.at[2, k], self.sems.at[3, k], chip_peer(k)
        )

    def start(self):
        for k in (1, 2, 3, 4, 5, 6, 7, 0):
            self.near(k).start()

    def send(self):
        for k in range(1, 8):
            self.near(k).wait_recv()
            base = (2 * lax.rem(self.chip + k, 8) + self.core) * SH

            @pl.loop(0, SH // 32)
            def _(i):
                rows = pl.ds(pl.multiple_of(base + i * 32, 32), 32)
                here = rows_at(i, 32)
                both = self.g_ref[rows, :].astype(F32) + self.sib_ref[k, here, :].astype(F32)
                self.out_ref[k - 1, here, :] = both.astype(BF16)

            self.far(k).start()

    def finish(self, result_ref):
        self.near(0).wait_recv()
        for k in range(1, 8):
            self.far(k).wait()
        base = self.s * SH

        @pl.loop(0, SH // 32)
        def _(i):
            rows = pl.ds(pl.multiple_of(base + i * 32, 32), 32)
            here = rows_at(i, 32)
            total = self.g_ref[rows, :].astype(F32) + self.sib_ref[0, here, :].astype(F32)
            for k in range(7):
                total = total + self.held_ref[k, here, :].astype(F32)
            result_ref[here, :] = total.astype(BF16)

        for k in range(8):
            self.near(k).wait_send()


def branch_end(x_ref, gate_ref, scatter, out_ref, base):
    @pl.loop(0, NT)
    def _(i):
        at = tile_at(i)
        value = x_ref[:, at].astype(F32) + gate_ref[:, at] * scatter.total(at)
        out_ref[pl.ds(base, OWN), at] = value.astype(BF16)


def input_grad(x_ref, dy_ref, gain_ref, scatter, sum_ref, out_ref, base):
    def moments(i, carry):
        squares, cross = carry
        at = tile_at(i)
        x = x_ref[:, at].astype(F32)
        weighted = scatter.total(at) * gain_ref[:, at]
        sum_ref[:, at] = weighted
        return squares + jnp.sum(x * x, -1, keepdims=True), cross + jnp.sum(x * weighted, -1, keepdims=True)

    zero = jnp.zeros((OWN, 1), F32)
    squares, cross = lax.fori_loop(0, NT, moments, (zero, zero))
    inverse = lax.rsqrt(squares / D + EPS)
    factor = inverse * inverse * inverse * (cross / D)

    @pl.loop(0, NT)
    def _(i):
        at = tile_at(i)
        value = dy_ref[:, at].astype(F32) + (inverse * sum_ref[:, at] - x_ref[:, at].astype(F32) * factor)
        out_ref[pl.ds(base, OWN), at] = value.astype(BF16)


def gather_kernel(proj_ref, outw_ref, w_ref, sems, local):
    greet(False, True, False)
    gather = Gather(proj_ref, outw_ref, w_ref, sems, local)
    gather.start()
    gather.relay()
    gather.finish()


def middle_kernel(
    part_ref, x_ref, gate_ref, proj_ref, outw_ref, middle_ref, w_ref,
    held_ref, own_ref, w_sems, local, rs_sems, swap_sems, ag_sems,
):
    _, f = place()
    greet(True, True, True)
    scatter = Scatter(part_ref, held_ref, rs_sems)
    scatter.start()
    gather = Gather(proj_ref, outw_ref, w_ref, w_sems, local)
    gather.start()
    scatter.wait()
    branch_end(x_ref, gate_ref, scatter, own_ref, 0)
    swap(own_ref, middle_ref, swap_sems, local.at[2])
    spread = Spread(middle_ref, ag_sems)
    spread.start()
    gather.relay()
    spread.wait()
    gather.finish()


def turn_kernel(
    part_ref, dpart_ref, g_ref, x_ref, dy_ref, gain_ref, gate_ref, grad_ref, mixed_ref, gsum_ref,
    held_ref, held2_ref, own_ref, sum_ref, sib_ref, gout_ref, gheld_ref,
    g_sems, local, rs_sems, rs2_sems, swap_sems, ag_sems, ag2_sems,
):
    _, f = place()
    greet(True, True, True)
    scatter = Scatter(dpart_ref, held_ref, rs_sems)
    scatter.start()
    reduce = Reduce(g_ref, sib_ref, gout_ref, gheld_ref, g_sems)
    reduce.start()
    scatter2 = Scatter(part_ref, held2_ref, rs2_sems)
    scatter2.start()
    reduce.send()
    scatter.wait()
    input_grad(x_ref, dy_ref, gain_ref, scatter, sum_ref, own_ref, 0)
    swap(own_ref, grad_ref, swap_sems, local)
    spread = Spread(grad_ref, ag_sems)
    spread.start()
    scatter2.wait()
    branch_end(x_ref, gate_ref, scatter2, mixed_ref, pl.multiple_of(f * OWN, OWN))
    spread2 = Spread(mixed_ref, ag2_sems)
    spread2.start()
    reduce.finish(gsum_ref)
    spread.wait()
    spread2.wait()


def last_kernel(
    dpart_ref, g_ref, x_ref, dy_ref, gain_ref, grad_ref, gsum_ref,
    held_ref, sum_ref, sib_ref, gout_ref, gheld_ref, g_sems, rs_sems, ag_sems,
):
    _, f = place()
    greet(True, True, False)
    scatter = Scatter(dpart_ref, held_ref, rs_sems)
    scatter.start()
    reduce = Reduce(g_ref, sib_ref, gout_ref, gheld_ref, g_sems)
    reduce.start()
    reduce.send()
    scatter.wait()
    input_grad(x_ref, dy_ref, gain_ref, scatter, sum_ref, grad_ref, pl.multiple_of(f * OWN, OWN))
    spread = Spread(grad_ref, ag_sems)
    spread.start()
    reduce.finish(gsum_ref)
    spread.wait()


VM = pl.BlockSpec(memory_space=pltpu.VMEM)
HBM = pl.BlockSpec(memory_space=pl.ANY)


def shaped(shape, dtype=BF16):
    return jax.ShapeDtypeStruct(shape, dtype)


def call(body, outs, scratch, collective_id=None, specs=None, name=None):
    extra = {} if collective_id is None else {"collective_id": collective_id, "has_side_effects": True}

    def run(*args):
        return pl.pallas_call(
            body,
            out_shape=outs,
            in_specs=specs or [VM] * len(args),
            out_specs=[VM] * len(outs),
            scratch_shapes=scratch,
            compiler_params=pltpu.CompilerParams(vmem_limit_bytes=VMEM_LIMIT, **extra),
            name=name,
        )(*args)

    return run


def sem(*shape):
    return pltpu.SemaphoreType.DMA(shape)


def local(clip_tokens, out_cotangent, proj_weight, out_weight, norm_gain, branch_gate, qk_gain):
    _, f = place()
    tokens = clip_tokens.reshape(T, D)
    cotangent = out_cotangent.reshape(T, D)
    outw = jnp.swapaxes(out_weight, 1, 2)
    gain = [norm_gain[b : b + 1] for b in range(2)]
    gate = [branch_gate[b : b + 1] for b in range(2)]
    own = lambda array: lax.dynamic_slice_in_dim(array, f * OWN, OWN, 0)
    grads = [pltpu.VMEM((8, SH, WC), BF16), pltpu.VMEM((7, SH, WC), BF16), pltpu.VMEM((7, SH, WC), BF16)]

    (w0,) = call(
        gather_kernel, [shaped((D, WC))], [sem(4, 8), sem(3)], 0, [HBM, HBM], name="gather_weights"
    )(proj_weight[0], outw[0])
    normed, projected, attended, part = call(
        spatial_forward,
        [shaped((T, D)), shaped((T, PC), F32), shaped((T, 2 * HD)), shaped((T, D))],
        [],
        name="spatial_forward",
    )(tokens, w0, gain[0], qk_gain[0])
    middle, w1 = call(
        middle_kernel,
        [shaped((T, D)), shaped((D, WC))],
        [pltpu.VMEM((7, OWN, D), BF16), pltpu.VMEM((OWN, D), BF16), sem(4, 8), sem(3), sem(2, 8), sem(2, 2), sem(2, 8)],
        1,
        [VM, VM, VM, HBM, HBM],
        name="to_positions",
    )(part, own(tokens), gate[0], proj_weight[1], outw[1])
    part, dpart, g1 = call(
        temporal_both,
        [shaped((T, D)), shaped((T, D)), shaped((D, WC))],
        [
            pltpu.VMEM((T, D), BF16),
            pltpu.VMEM((T, PC), F32),
            pltpu.VMEM((T, 2 * HD), BF16),
            pltpu.VMEM((T, 2 * HD), F32),
            pltpu.VMEM((T, PC), BF16),
        ],
        name="temporal_both",
    )(middle, cotangent, w1, gain[1], gate[1], qk_gain[1])
    grad_frames, mixed, gsum1 = call(
        turn_kernel,
        [shaped((T, D)), shaped((T, D)), shaped((SH, WC))],
        [
            pltpu.VMEM((7, OWN, D), BF16),
            pltpu.VMEM((7, OWN, D), BF16),
            pltpu.VMEM((OWN, D), BF16),
            pltpu.VMEM((OWN, D), F32),
            *grads,
            sem(4, 8),
            pltpu.SemaphoreType.DMA,
            sem(2, 8),
            sem(2, 8),
            sem(2, 2),
            sem(2, 8),
            sem(2, 8),
        ],
        2,
        name="to_frames",
    )(part, dpart, g1, own(middle), own(cotangent), gain[1], gate[1])
    dpart, g0 = call(
        spatial_backward,
        [shaped((T, D)), shaped((D, WC))],
        [pltpu.VMEM((T, 2 * HD), F32), pltpu.VMEM((T, PC), BF16)],
        name="spatial_backward",
    )(grad_frames, w0, gate[0], qk_gain[0], normed, projected, attended)
    grad_clip, gsum0 = call(
        last_kernel,
        [shaped((T, D)), shaped((SH, WC))],
        [
            pltpu.VMEM((7, OWN, D), BF16),
            pltpu.VMEM((OWN, D), F32),
            *grads,
            sem(4, 8),
            sem(2, 8),
            sem(2, 8),
        ],
        3,
        name="clip_gradient",
    )(dpart, g0, own(tokens), own(grad_frames), gain[0])
    grad_proj = jnp.stack([gsum0[:, :PC], gsum1[:, :PC]])
    grad_outw = jnp.swapaxes(jnp.stack([gsum0[:, PC:], gsum1[:, PC:]]), 1, 2)
    return (mixed.reshape(16, 16, D), grad_clip.reshape(1, T, D), grad_proj, grad_outw)


def solution(mesh):
    placed = (
        P("seq", None, None),
        P(None, "seq", None),
        P(None, "seq", "fsdp"),
        P(None, "fsdp", "seq"),
        P(),
        P(),
        P(),
    )
    return jax.shard_map(
        local,
        mesh=mesh,
        in_specs=placed,
        out_specs=(
            P(None, "seq", None),
            P("seq", None, None),
            P(None, "seq", "fsdp"),
            P(None, "fsdp", "seq"),
        ),
        check_vma=False,
    )
```

```python
import functools

import jax
import jax.numpy as jnp
from jax import lax
from jax.experimental import pallas as pl
from jax.experimental.pallas import tpu as pltpu
from jax.sharding import PartitionSpec as P

EPS = 1e-06
MESH = pl.DeviceIdType.MESH
D = 3584
HD = 128
T = 256
OWN = 32
GROUP = 896
SH = 224
WC = 1024
PC = 768
TILE = 512
NT = D // TILE
F32 = jnp.float32
BF16 = jnp.bfloat16
VMEM_LIMIT = 60 * 1024 * 1024


def tile_at(i, size=TILE):
    return pl.ds(pl.multiple_of(i * size, size), size)


def dot(a, b, contract=((1,), (0,))):
    return lax.dot_general(a, b, (contract, ((), ())), preferred_element_type=F32)


def head_forward(proj_ref, qkg, head, temporal):
    base = head * 3 * HD
    q_raw = proj_ref[:, base : base + HD]
    k_raw = proj_ref[:, base + HD : base + 2 * HD]
    q_inv = lax.rsqrt(jnp.mean(q_raw * q_raw, -1, keepdims=True) + EPS)
    k_inv = lax.rsqrt(jnp.mean(k_raw * k_raw, -1, keepdims=True) + EPS)
    q = (q_raw * q_inv * qkg[0:1, :]).astype(BF16)
    k = (k_raw * k_inv * qkg[1:2, :]).astype(BF16)
    v = proj_ref[:, base + 2 * HD : base + 3 * HD].astype(BF16)
    scores = dot(q, k, ((1,), (1,))) * HD**-0.5
    if temporal:
        rows = lax.broadcasted_iota(jnp.int32, (T, T), 0)
        cols = lax.broadcasted_iota(jnp.int32, (T, T), 1)
        scores = jnp.where((rows & 15) == (cols & 15), scores, -1e30)
    top = jnp.max(scores, -1, keepdims=True)
    grown = jnp.exp(scores - top)
    probs = grown / jnp.sum(grown, -1, keepdims=True)
    return q_raw, k_raw, q_inv, k_inv, q, k, v, probs


def head_backward(proj_ref, qkg, head, temporal, d_att, dproj_ref):
    q_raw, k_raw, q_inv, k_inv, q, k, v, probs = head_forward(proj_ref, qkg, head, temporal)
    base = head * 3 * HD
    rounded = probs.astype(BF16)
    d_probs = dot(d_att, v, ((1,), (1,))).astype(BF16).astype(F32)
    d_v = dot(rounded, d_att, ((0,), (0,)))
    d_scores = probs * (d_probs - jnp.sum(probs * d_probs, -1, keepdims=True))
    d_scores = (d_scores * HD**-0.5).astype(BF16)
    d_q = dot(d_scores, k).astype(BF16).astype(F32) * qkg[0:1, :]
    d_k = dot(d_scores, q, ((0,), (0,))).astype(BF16).astype(F32) * qkg[1:2, :]
    d_q = q_inv * d_q - q_raw * (q_inv * q_inv * q_inv) * jnp.mean(q_raw * d_q, -1, keepdims=True)
    d_k = k_inv * d_k - k_raw * (k_inv * k_inv * k_inv) * jnp.mean(k_raw * d_k, -1, keepdims=True)
    dproj_ref[:, base : base + HD] = d_q.astype(BF16)
    dproj_ref[:, base + HD : base + 2 * HD] = d_k.astype(BF16)
    dproj_ref[:, base + 2 * HD : base + 3 * HD] = d_v.astype(BF16)


def inverse_norm(x_ref):
    def square(i, total):
        x = x_ref[:, tile_at(i)].astype(F32)
        return total + jnp.sum(x * x, -1, keepdims=True)

    total = lax.fori_loop(0, NT, square, jnp.zeros((T, 1), F32))
    return lax.rsqrt(total / D + EPS)


def normalise(x_ref, gain, normed_ref):
    inverse = inverse_norm(x_ref)

    @pl.loop(0, NT)
    def _(i):
        at = tile_at(i)
        normed_ref[:, at] = (x_ref[:, at].astype(F32) * inverse * gain[:, at]).astype(BF16)


def project(group, normed_ref, w_ref, proj_ref, first):
    at = tile_at(group, GROUP)
    product = dot(normed_ref[:, at], w_ref[at, :PC])
    if first:
        proj_ref[...] = product
    else:
        proj_ref[...] += product


def branch(proj_ref, qkg, w_ref, att_ref, part_ref, temporal):
    for head in range(2):
        parts = head_forward(proj_ref, qkg, head, temporal)
        att_ref[:, head * HD : (head + 1) * HD] = dot(parts[7].astype(BF16), parts[6]).astype(BF16)
    att = att_ref[...]

    @pl.loop(0, NT)
    def _(i):
        at = tile_at(i)
        part_ref[:, at] = dot(att, w_ref[at, PC:], ((1,), (1,))).astype(BF16)


def scaled_tile(dy_ref, gate, at):
    return (dy_ref[:, at].astype(F32) * gate[:, at]).astype(BF16)


def backward(dy_ref, w_ref, gate, qkg, proj_ref, dpart_ref, datt_ref, dproj_ref, temporal):
    datt_ref[...] = jnp.zeros_like(datt_ref)

    @pl.loop(0, NT)
    def _(i):
        at = tile_at(i)
        datt_ref[...] += dot(scaled_tile(dy_ref, gate, at), w_ref[at, PC:])

    for head in range(2):
        d_att = datt_ref[:, head * HD : (head + 1) * HD].astype(BF16)
        head_backward(proj_ref, qkg, head, temporal, d_att, dproj_ref)
    dproj = dproj_ref[...]

    @pl.loop(0, NT)
    def _(i):
        at = tile_at(i)
        dpart_ref[:, at] = dot(dproj, w_ref[at, :PC], ((1,), (1,))).astype(BF16)


def weight_grads(dy_ref, gate, normed_ref, att_ref, dproj_ref, g_ref):
    dproj = dproj_ref[...]
    att = att_ref[...]

    @pl.loop(0, NT)
    def _(i):
        at = tile_at(i)
        g_ref[at, :PC] = dot(normed_ref[:, at], dproj, ((0,), (0,))).astype(BF16)
        g_ref[at, PC:] = dot(scaled_tile(dy_ref, gate, at), att, ((0,), (0,))).astype(BF16)


def place():
    return lax.axis_index("seq"), lax.axis_index("fsdp")


def remote(src, dst, send, recv, device):
    return pltpu.make_async_remote_copy(
        src_ref=src, dst_ref=dst, send_sem=send, recv_sem=recv, device_id=device, device_id_type=MESH
    )


def sibling():
    s, f = place()
    return (s + 1 - 2 * lax.rem(s, 2), f)


def seq_node(dp, dq):
    s, f = place()
    node = 2 * lax.rem(s // 4 + dp + 4, 4) + lax.rem(s // 2 + dq, 2)
    s_there = 2 * node + lax.rem(s, 2)
    return (s_there, f), s_there * SH


def fsdp_node(dp, dq):
    s, f = place()
    return (s, 2 * lax.rem(f // 2 + dp + 4, 4) + lax.rem(f + dq, 2))


def by_frames(dp, dq):
    device = fsdp_node(dp, dq)
    return device, device[1] * OWN


def by_positions(dp, dq):
    s, _ = place()
    device = fsdp_node(dp, dq)
    shifted = 2 * lax.rem(device[1] // 2 + s // 4, 4) + lax.rem(device[1], 2)
    return device, shifted * OWN


def swap_out():
    s, _ = place()
    pair = by_positions(0, 0)[1] // OWN
    return [(2 * pair + e, s // 2) for e in range(2)]


def swap_back():
    s, f = place()
    there = 2 * lax.rem(s // 4 - f // 2 + 4, 4) + lax.rem(s // 2, 2)
    return [(2 * f + i, there) for i in range(2)]


def is_me(device):
    s, f = place()
    return jnp.logical_and(device[0] == s, device[1] == f)


def greet():
    barrier = pltpu.get_barrier_semaphore()
    peers = [sibling()]
    for dp, dq in ((1, 0), (-1, 0), (0, 1)):
        peers += [seq_node(dp, dq)[0], fsdp_node(dp, dq)]
    for peer in peers:
        pl.semaphore_signal(barrier, inc=1, device_id=peer, device_id_type=MESH)
    count = len(peers)
    for peer in swap_out() + swap_back():
        other = jnp.logical_not(is_me(peer))
        count = count + other.astype(jnp.int32)

        @pl.when(other)
        def _():
            pl.semaphore_signal(barrier, inc=1, device_id=peer, device_id_type=MESH)

    pl.semaphore_wait(barrier, count)


def rows_at(start, n):
    return pl.ds(pl.multiple_of(start, 16), n)


class Gather:
    MESSAGES = (
        ((0, 0), None, (1, 0)),
        ((0, 0), None, (-1, 0)),
        ((0, 0), None, (0, 1)),
        ((-1, 0), 0, (1, 0)),
        ((1, 0), 1, (-1, 0)),
        ((0, 1), None, (1, 0)),
        ((0, 1), None, (-1, 0)),
        ((2, 0), 0, (0, 1)),
        ((2, 0), 1, (0, 1)),
    )

    def __init__(self, ref, node, size, sems):
        self.ref, self.node, self.size, self.sems = ref, node, size, sems

    def copy(self, m):
        shard, half, target = self.MESSAGES[m]
        start, n = self.node(*shard)[1], self.size
        if half is not None:
            n = n // 2
            start = start + half * n
        rows = self.ref.at[rows_at(start, n)]
        return remote(rows, rows, self.sems.at[0, m], self.sems.at[1, m], self.node(*target)[0])

    def send(self, *messages):
        for m in messages:
            self.copy(m).start()

    def got(self, *messages):
        for m in messages:
            self.copy(m).wait_recv()

    def start(self):
        self.send(0, 1, 2)

    def middle(self):
        self.got(0)
        self.send(3)
        self.got(1)
        self.send(4)
        self.got(2)
        self.send(5, 6)

    def last(self):
        self.got(3)
        self.send(7)
        self.got(4)
        self.send(8)

    def end(self):
        self.got(5, 6, 7, 8)
        self.sent()

    def sent(self):
        for m in range(9):
            self.copy(m).wait_send()


class Weights(Gather):
    SHARDS = ((0, 0), (-1, 0), (1, 0), (0, 1), (2, 0), (-1, 1), (1, 1), (2, 1))

    def __init__(self, block, proj_ref, outw_ref, w_ref, sems, near_sems, local):
        super().__init__(w_ref, seq_node, SH, sems)
        self.near_sems = near_sems
        rows = rows_at(seq_node(0, 0)[1], SH)
        self.own = [
            pltpu.make_async_copy(proj_ref.at[block], w_ref.at[rows, pl.ds(0, PC)], local.at[0]),
            pltpu.make_async_copy(outw_ref.at[block], w_ref.at[rows, pl.ds(PC, WC - PC)], local.at[1]),
        ]

    def near(self, n):
        rows = self.ref.at[rows_at(self.node(*self.SHARDS[n])[1], SH)]
        return remote(rows, rows, self.near_sems.at[0, n], self.near_sems.at[1, n], sibling())

    def near_got(self, *shards):
        for n in shards:
            self.near(n).wait_recv()

    def load(self):
        for copy in self.own:
            copy.start()

    def start(self):
        for copy in self.own:
            copy.wait()
        super().start()
        self.near(0).start()

    def middle(self):
        self.got(0)
        self.send(3)
        self.near(1).start()
        self.got(1)
        self.send(4)
        self.near(2).start()
        self.got(2)
        self.send(5, 6)
        self.near(3).start()

    def last(self):
        super().last()
        self.near(4).start()

    def fifth(self):
        self.got(5)
        self.near(5).start()
        self.got(6)
        self.near(6).start()

    def end(self):
        self.got(7, 8)
        self.near(7).start()

    def sent(self):
        super().sent()
        for n in range(8):
            self.near(n).wait_send()


def add_rows(ref, start, n, stage):
    @pl.loop(0, n // 16)
    def _(i):
        rows, here = rows_at(start + i * 16, 16), rows_at(i * 16, 16)
        ref[rows, :] = (ref[rows, :].astype(F32) + stage[here, :].astype(F32)).astype(BF16)


class Reduce:
    MESSAGES = (
        ((-1, 0), None, (-1, 0), 5),
        ((1, 0), None, (1, 0), 6),
        ((0, 1), None, (0, 1), 4),
        ((2, 0), 0, (-1, 0), 3),
        ((2, 0), 1, (1, 0), 3),
        ((-1, 1), None, (-1, 0), 1),
        ((1, 1), None, (1, 0), 2),
        ((2, 1), None, (0, 1), 0),
    )

    def __init__(self, ref, node, size, held, sems):
        self.ref, self.node, self.size, self.held, self.sems = ref, node, size, held, sems

    def copy(self, m):
        shard, half, target, slot = self.MESSAGES[m]
        start, n, first = self.node(*shard)[1], self.size, 0
        if half is not None:
            n = n // 2
            first = half * n
        src = self.ref.at[rows_at(start + first, n)]
        dst = self.held.at[pl.ds(slot * self.size + first, n)]
        return remote(src, dst, self.sems.at[0, m], self.sems.at[1, m], self.node(*target)[0])

    def send(self, *messages):
        for m in messages:
            self.copy(m).start()

    def got(self, *messages):
        for m in messages:
            self.copy(m).wait_recv()

    def add(self, shard, slot, half=None):
        start, n, first = self.node(*shard)[1], self.size, 0
        if half is not None:
            n = n // 2
            first = half * n
        add_rows(self.ref, start + first, n, self.held.at[pl.ds(slot * self.size + first, n)])

    def ready(self, *shards):
        pass

    def start(self):
        self.ready(0, 1, 2)
        self.send(7, 5, 6)

    def middle(self):
        self.ready(3)
        self.got(7)
        self.add((2, 0), 0)
        self.send(3, 4)
        self.ready(4)
        self.got(5)
        self.add((0, 1), 1)
        self.got(6)
        self.add((0, 1), 2)
        self.send(2)

    def last(self):
        self.ready(5)
        self.got(3)
        self.add((-1, 0), 3, 0)
        self.send(0)
        self.ready(6)
        self.got(4)
        self.add((1, 0), 3, 1)
        self.send(1)

    def end(self):
        self.ready(7)
        self.got(0, 1, 2)
        for m in range(8):
            self.copy(m).wait_send()

    def total(self, at):
        summed = self.ref[rows_at(self.node(0, 0)[1], self.size), at].astype(F32)
        for slot in (4, 5, 6):
            summed = summed + self.held[pl.ds(slot * self.size, self.size), at].astype(F32)
        return summed


class WeightGrads(Reduce):
    SHARDS = ((2, 1), (-1, 1), (1, 1), (2, 0), (0, 1), (-1, 0), (1, 0), (0, 0))

    def __init__(self, ref, held, sems, near_held, near_sems):
        super().__init__(ref, seq_node, SH, held, sems)
        self.near_held, self.near_sems = near_held, near_sems

    def near(self, n):
        s, _ = place()
        start = self.node(*self.SHARDS[n])[1] + (1 - 2 * lax.rem(s, 2)) * SH
        return remote(
            self.ref.at[rows_at(start, SH)], self.near_held.at[pl.ds(n * SH, SH)],
            self.near_sems.at[0, n], self.near_sems.at[1, n], sibling(),
        )

    def ready(self, *shards):
        for n in shards:
            self.near(n).wait_recv()
            add_rows(self.ref, self.node(*self.SHARDS[n])[1], SH, self.near_held.at[pl.ds(n * SH, SH)])

    def pair(self):
        for n in range(8):
            self.near(n).start()

    def result(self, block, gproj_ref, goutw_ref):
        base = self.node(0, 0)[1]

        @pl.loop(0, SH // 16)
        def _(i):
            rows, here = rows_at(base + i * 16, 16), rows_at(i * 16, 16)
            total = self.ref[rows, :].astype(F32)
            for slot in (4, 5, 6):
                total = total + self.held[rows_at(slot * SH + i * 16, 16), :].astype(F32)
            gproj_ref[block, here, :] = total[:, :PC].astype(BF16)
            goutw_ref[block, here, :] = total[:, PC:].astype(BF16)

        for n in range(8):
            self.near(n).wait_send()


class Swap:
    def __init__(self, src_ref, dst_ref, targets, sources, base, sems, local):
        self.src_ref, self.dst_ref, self.targets, self.base = src_ref, dst_ref, targets, base
        self.sources, self.sems, self.local = sources, sems, local

    def each(self, act):
        s, _ = place()
        for j in range(2):
            src = self.src_ref.at[pl.ds(j * 16, 16)]
            there = self.dst_ref.at[rows_at(s * 16, 16)]
            here = self.dst_ref.at[rows_at(self.base + j * 16, 16)]
            act(j, src, there, here)

    def start(self):
        s, _ = place()

        def act(j, src, there, here):
            mine = is_me(self.targets[j])

            @pl.when(mine)
            def _():
                pltpu.make_async_copy(src, here, self.local).start()

            @pl.when(jnp.logical_not(mine))
            def _():
                remote(src, there, self.sems.at[0, j], self.sems.at[1, lax.rem(s, 2)], self.targets[j]).start()

        self.each(act)

    def wait(self):
        def act(j, src, there, here):
            mine = is_me(self.targets[j])
            copy = lambda: remote(src, here, self.sems.at[0, j], self.sems.at[1, j], self.targets[j])

            @pl.when(mine)
            def _():
                pltpu.make_async_copy(src, here, self.local).wait()

            @pl.when(jnp.logical_not(mine))
            def _():
                copy().wait_send()
                copy().wait_recv()

        self.each(act)


def branch_end(x_ref, x_base, gate, reduced, out_ref):
    @pl.loop(0, NT)
    def _(i):
        at = tile_at(i)
        value = x_ref[rows_at(x_base, OWN), at].astype(F32) + gate[:, at] * reduced.total(at)
        out_ref[:, at] = value.astype(BF16)


def input_grad(x_ref, x_base, dy_ref, dy_base, gain, reduced, sum_ref, out_ref):
    def moments(i, carry):
        squares, cross = carry
        at = tile_at(i)
        x = x_ref[rows_at(x_base, OWN), at].astype(F32)
        weighted = reduced.total(at) * gain[:, at]
        sum_ref[:, at] = weighted
        return squares + jnp.sum(x * x, -1, keepdims=True), cross + jnp.sum(x * weighted, -1, keepdims=True)

    zero = jnp.zeros((OWN, 1), F32)
    squares, cross = lax.fori_loop(0, NT, moments, (zero, zero))
    inverse = lax.rsqrt(squares / D + EPS)
    factor = inverse * inverse * inverse * (cross / D)

    @pl.loop(0, NT)
    def _(i):
        at = tile_at(i)
        x = x_ref[rows_at(x_base, OWN), at].astype(F32)
        value = dy_ref[rows_at(dy_base, OWN), at].astype(F32) + (inverse * sum_ref[:, at] - x * factor)
        out_ref[:, at] = value.astype(BF16)


def whole(
    x_ref, dy_ref, proj_in, outw_in, gain_ref, gate_ref, qkg_ref,
    mixed_ref, clip_ref, gproj_ref, goutw_ref,
    w0_ref, w1_ref, g_ref, normed0_ref, normed1_ref, proj0_ref, proj1_ref, att0_ref, att1_ref, datt_ref, dproj_ref,
    part_ref, part1_ref, middle_ref, grad_ref, held_ref, own_ref, sum_ref, near1_ref, far1_ref,
    w_sems, wn_sems, local, rs_sems, ag_sems, g_sems, gn_sems, swap_sems,
):
    s, f = place()
    x_group = s // 4
    gain0, gain1, gate0, gate1 = (r.at[pl.ds(b, 1)] for r in (gain_ref, gate_ref) for b in range(2))
    qkg0, qkg1 = qkg_ref[0], qkg_ref[1]
    w0 = Weights(0, proj_in, outw_in, w0_ref, w_sems.at[0], wn_sems.at[0], local.at[0])
    w1 = Weights(1, proj_in, outw_in, w1_ref, w_sems.at[1], wn_sems.at[1], local.at[1])
    positions, frames = by_positions(0, 0)[1], by_frames(0, 0)[1]

    w0.load()
    w1.load()
    greet()
    w0.start()
    normalise(x_ref, gain0, normed0_ref)
    w0.middle()
    w0.near_got(0, 3)
    project(x_group, normed0_ref, w0_ref, proj0_ref, True)
    w0.last()
    w0.fifth()
    w1.start()
    w0.near_got(1, 5)
    project(lax.rem(x_group + 3, 4), normed0_ref, w0_ref, proj0_ref, False)
    w0.near_got(2, 6)
    project(lax.rem(x_group + 1, 4), normed0_ref, w0_ref, proj0_ref, False)
    w0.end()
    w0.near_got(4, 7)
    project(lax.rem(x_group + 2, 4), normed0_ref, w0_ref, proj0_ref, False)
    branch(proj0_ref, qkg0, w0_ref, att0_ref, part_ref, False)

    r0 = Reduce(part_ref, by_positions, OWN, held_ref.at[0], rs_sems.at[0])
    r0.start()
    w1.middle()
    r0.middle()
    r0.last()
    w1.last()
    r0.end()
    branch_end(x_ref, positions, gate0, r0, own_ref.at[0])
    out = Swap(own_ref.at[0], middle_ref, swap_out(), None, frames, swap_sems.at[0], local.at[2, 0])
    out.start()
    w1.fifth()
    out.wait()
    a0 = Gather(middle_ref, by_frames, OWN, ag_sems.at[0])
    a0.start()
    w1.end()
    a0.middle()
    a0.last()
    w0.sent()
    w1.sent()
    w1.near_got(0, 1, 2, 3, 4, 5, 6, 7)
    a0.end()

    normalise(middle_ref, gain1, normed1_ref)
    for group in range(4):
        project(group, normed1_ref, w1_ref, proj1_ref, group == 0)
    branch(proj1_ref, qkg1, w1_ref, att1_ref, part1_ref, True)
    r1 = Reduce(part1_ref, by_frames, OWN, held_ref.at[1], rs_sems.at[1])
    r1.start()
    backward(dy_ref, w1_ref, gate1, qkg1, proj1_ref, part_ref, datt_ref, dproj_ref, True)

    r2 = Reduce(part_ref, by_frames, OWN, held_ref.at[2], rs_sems.at[2])
    r2.start()
    r1.middle()
    weight_grads(dy_ref, gate1, normed1_ref, att1_ref, dproj_ref, g_ref)
    grads1 = WeightGrads(g_ref, far1_ref, g_sems.at[1], near1_ref, gn_sems.at[1])
    grads1.pair()
    r2.middle()
    r1.last()
    r2.last()
    grads1.start()
    r2.end()
    input_grad(middle_ref, frames, dy_ref, frames, gain1, r2, sum_ref, own_ref.at[1])
    back = Swap(own_ref.at[1], grad_ref, swap_back(), None, positions, swap_sems.at[1], local.at[2, 0])
    back.start()
    r1.end()
    branch_end(middle_ref, frames, gate1, r1, own_ref.at[2])
    keep = pltpu.make_async_copy(own_ref.at[2], mixed_ref.at[rows_at(frames, OWN)], local.at[2, 1])
    keep.start()
    back.wait()
    a1 = Gather(grad_ref, by_positions, OWN, ag_sems.at[1])
    a1.start()
    grads1.middle()
    a1.middle()
    grads1.last()
    a1.last()
    keep.wait()
    a2 = Gather(mixed_ref, by_frames, OWN, ag_sems.at[2])
    a2.start()
    grads1.end()
    grads1.result(1, gproj_ref, goutw_ref)
    a1.end()

    backward(grad_ref, w0_ref, gate0, qkg0, proj0_ref, part_ref, datt_ref, dproj_ref, False)
    r3 = Reduce(part_ref, by_positions, OWN, held_ref.at[3], rs_sems.at[3])
    r3.start()
    a2.middle()
    weight_grads(grad_ref, gate0, normed0_ref, att0_ref, dproj_ref, g_ref)
    near0_ref, far0_ref = w1_ref.at[pl.ds(0, 8 * SH)], w1_ref.at[pl.ds(8 * SH, 7 * SH)]
    grads0 = WeightGrads(g_ref, far0_ref, g_sems.at[0], near0_ref, gn_sems.at[0])
    grads0.pair()
    r3.middle()
    r3.last()
    grads0.start()
    a2.last()
    r3.end()
    input_grad(x_ref, positions, grad_ref, positions, gain0, r3, sum_ref, own_ref.at[3])
    keep = pltpu.make_async_copy(own_ref.at[3], clip_ref.at[rows_at(positions, OWN)], local.at[2, 1])
    keep.start()
    keep.wait()
    a3 = Gather(clip_ref, by_positions, OWN, ag_sems.at[3])
    a3.start()
    grads0.middle()
    a3.middle()
    grads0.last()
    a3.last()
    a2.end()
    grads0.end()
    grads0.result(0, gproj_ref, goutw_ref)
    a3.end()


def shaped(shape, dtype=BF16):
    return jax.ShapeDtypeStruct(shape, dtype)


def sem(*shape):
    return pltpu.SemaphoreType.DMA(shape)


def local_program(clip_tokens, out_cotangent, proj_weight, out_weight, norm_gain, branch_gate, qk_gain):
    in_vmem = pl.BlockSpec(memory_space=pltpu.VMEM)
    anywhere = pl.BlockSpec(memory_space=pl.ANY)
    tokens = lambda *lead: pltpu.VMEM((*lead, T, D), BF16)
    mixed, clip, gproj, goutw = pl.pallas_call(
        whole,
        out_shape=[shaped((T, D)), shaped((T, D)), shaped((2, SH, PC)), shaped((2, SH, WC - PC))],
        in_specs=[in_vmem, in_vmem, anywhere, anywhere, in_vmem, in_vmem, in_vmem],
        out_specs=[anywhere, anywhere, in_vmem, in_vmem],
        scratch_shapes=[
            pltpu.VMEM((D, WC), BF16),
            pltpu.VMEM((D, WC), BF16),
            pltpu.VMEM((D, WC), BF16),
            tokens(),
            tokens(),
            pltpu.VMEM((T, PC), F32),
            pltpu.VMEM((T, PC), F32),
            pltpu.VMEM((T, 2 * HD), BF16),
            pltpu.VMEM((T, 2 * HD), BF16),
            pltpu.VMEM((T, 2 * HD), F32),
            pltpu.VMEM((T, PC), BF16),
            tokens(),
            tokens(),
            tokens(),
            tokens(),
            pltpu.VMEM((4, 7 * OWN, D), BF16),
            pltpu.VMEM((4, OWN, D), BF16),
            pltpu.VMEM((OWN, D), F32),
            pltpu.VMEM((8 * SH, WC), BF16),
            pltpu.VMEM((7 * SH, WC), BF16),
            sem(2, 2, 9),
            sem(2, 2, 8),
            sem(3, 2),
            sem(4, 2, 8),
            sem(4, 2, 9),
            sem(2, 2, 8),
            sem(2, 2, 8),
            sem(2, 2, 2),
        ],
        compiler_params=pltpu.CompilerParams(
            vmem_limit_bytes=VMEM_LIMIT, collective_id=0, has_side_effects=True
        ),
        name="two_blocks",
    )(
        clip_tokens.reshape(T, D),
        out_cotangent.reshape(T, D),
        proj_weight,
        jnp.swapaxes(out_weight, 1, 2),
        norm_gain,
        branch_gate,
        qk_gain,
    )
    return mixed.reshape(16, 16, D), clip.reshape(1, T, D), gproj, jnp.swapaxes(goutw, 1, 2)


def solution(mesh):
    placed = (
        P("seq", None, None),
        P(None, "seq", None),
        P(None, "seq", "fsdp"),
        P(None, "fsdp", "seq"),
        P(),
        P(),
        P(),
    )
    return jax.shard_map(
        local_program,
        mesh=mesh,
        in_specs=placed,
        out_specs=(
            P(None, "seq", None),
            P("seq", None, None),
            P(None, "seq", "fsdp"),
            P(None, "fsdp", "seq"),
        ),
        check_vma=False,
    )
```

```python
import functools

import jax
import jax.numpy as jnp
from jax import lax
from jax.experimental import pallas as pl
from jax.experimental.pallas import tpu as pltpu
from jax.sharding import PartitionSpec as P

EPS = 1e-06
MESH = pl.DeviceIdType.MESH
D = 3584
HD = 128
T = 256
OWN = 32
GROUP = 896
SH = 224
WC = 1024
PC = 768
TILE = 512
NT = D // TILE
F32 = jnp.float32
BF16 = jnp.bfloat16
VMEM_LIMIT = 60 * 1024 * 1024


def tile_at(i, size=TILE):
    return pl.ds(pl.multiple_of(i * size, size), size)


def dot(a, b, contract=((1,), (0,))):
    return lax.dot_general(a, b, (contract, ((), ())), preferred_element_type=F32)


def head_forward(proj_ref, qkg, head, temporal):
    base = head * 3 * HD
    q_raw = proj_ref[:, base : base + HD]
    k_raw = proj_ref[:, base + HD : base + 2 * HD]
    q_inv = lax.rsqrt(jnp.mean(q_raw * q_raw, -1, keepdims=True) + EPS)
    k_inv = lax.rsqrt(jnp.mean(k_raw * k_raw, -1, keepdims=True) + EPS)
    q = (q_raw * q_inv * qkg[0:1, :]).astype(BF16)
    k = (k_raw * k_inv * qkg[1:2, :]).astype(BF16)
    v = proj_ref[:, base + 2 * HD : base + 3 * HD].astype(BF16)
    scores = dot(q, k, ((1,), (1,))) * HD**-0.5
    if temporal:
        rows = lax.broadcasted_iota(jnp.int32, (T, T), 0)
        cols = lax.broadcasted_iota(jnp.int32, (T, T), 1)
        scores = jnp.where((rows & 15) == (cols & 15), scores, -1e30)
    top = jnp.max(scores, -1, keepdims=True)
    grown = jnp.exp(scores - top)
    probs = grown / jnp.sum(grown, -1, keepdims=True)
    return q_raw, k_raw, q_inv, k_inv, q, k, v, probs


def head_backward(proj_ref, qkg, head, temporal, d_att, dproj_ref):
    q_raw, k_raw, q_inv, k_inv, q, k, v, probs = head_forward(proj_ref, qkg, head, temporal)
    base = head * 3 * HD
    rounded = probs.astype(BF16)
    d_probs = dot(d_att, v, ((1,), (1,))).astype(BF16).astype(F32)
    d_v = dot(rounded, d_att, ((0,), (0,)))
    d_scores = probs * (d_probs - jnp.sum(probs * d_probs, -1, keepdims=True))
    d_scores = (d_scores * HD**-0.5).astype(BF16)
    d_q = dot(d_scores, k).astype(BF16).astype(F32) * qkg[0:1, :]
    d_k = dot(d_scores, q, ((0,), (0,))).astype(BF16).astype(F32) * qkg[1:2, :]
    d_q = q_inv * d_q - q_raw * (q_inv * q_inv * q_inv) * jnp.mean(q_raw * d_q, -1, keepdims=True)
    d_k = k_inv * d_k - k_raw * (k_inv * k_inv * k_inv) * jnp.mean(k_raw * d_k, -1, keepdims=True)
    dproj_ref[:, base : base + HD] = d_q.astype(BF16)
    dproj_ref[:, base + HD : base + 2 * HD] = d_k.astype(BF16)
    dproj_ref[:, base + 2 * HD : base + 3 * HD] = d_v.astype(BF16)


def inverse_norm(x_ref):
    def square(i, total):
        x = x_ref[:, tile_at(i)].astype(F32)
        return total + jnp.sum(x * x, -1, keepdims=True)

    total = lax.fori_loop(0, NT, square, jnp.zeros((T, 1), F32))
    return lax.rsqrt(total / D + EPS)


def normalise(x_ref, gain, normed_ref):
    inverse = inverse_norm(x_ref)

    @pl.loop(0, NT)
    def _(i):
        at = tile_at(i)
        normed_ref[:, at] = (x_ref[:, at].astype(F32) * inverse * gain[:, at]).astype(BF16)


def project(group, normed_ref, w_ref, proj_ref, first):
    at = tile_at(group, GROUP)
    product = dot(normed_ref[:, at], w_ref[at, :PC])
    if first:
        proj_ref[...] = product
    else:
        proj_ref[...] += product


def attend(proj_ref, qkg, att_ref, temporal):
    for head in range(2):
        parts = head_forward(proj_ref, qkg, head, temporal)
        att_ref[:, head * HD : (head + 1) * HD] = dot(parts[7].astype(BF16), parts[6]).astype(BF16)


def branch(att_ref, w_ref, part_ref, cols):
    att = att_ref[...]

    @pl.loop(cols[0] // TILE, sum(cols) // TILE)
    def _(i):
        at = tile_at(i)
        part_ref[:, at] = dot(att, w_ref[at, PC:], ((1,), (1,))).astype(BF16)


def scaled_tile(dy_ref, gate, at):
    return (dy_ref[:, at].astype(F32) * gate[:, at]).astype(BF16)


def attended_grad(dy_ref, w_ref, gate, datt_ref):
    datt_ref[...] = jnp.zeros_like(datt_ref)

    @pl.loop(0, NT)
    def _(i):
        at = tile_at(i)
        datt_ref[...] += dot(scaled_tile(dy_ref, gate, at), w_ref[at, PC:])


def projected_grad(qkg, proj_ref, datt_ref, dproj_ref, temporal):
    for head in range(2):
        d_att = datt_ref[:, head * HD : (head + 1) * HD].astype(BF16)
        head_backward(proj_ref, qkg, head, temporal, d_att, dproj_ref)


def normed_grad(dproj_ref, w_ref, dpart_ref, cols):
    dproj = dproj_ref[...]

    @pl.loop(cols[0] // TILE, sum(cols) // TILE)
    def _(i):
        at = tile_at(i)
        dpart_ref[:, at] = dot(dproj, w_ref[at, :PC], ((1,), (1,))).astype(BF16)


def proj_grads(normed_ref, dproj_ref, g_ref, cols):
    to = pl.ds(*cols)
    dproj = dproj_ref[:, to]

    @pl.loop(0, NT)
    def _(i):
        at = tile_at(i)
        g_ref[at, to] = dot(normed_ref[:, at], dproj, ((0,), (0,))).astype(BF16)


def outw_grads(dy_ref, gate, att_ref, g_ref):
    att = att_ref[...]

    @pl.loop(0, NT)
    def _(i):
        at = tile_at(i)
        g_ref[at, PC:] = dot(scaled_tile(dy_ref, gate, at), att, ((0,), (0,))).astype(BF16)


def place():
    return lax.axis_index("seq"), lax.axis_index("fsdp")


def remote(src, dst, send, recv, device):
    return pltpu.make_async_remote_copy(
        src_ref=src, dst_ref=dst, send_sem=send, recv_sem=recv, device_id=device, device_id_type=MESH
    )


def sibling():
    s, f = place()
    return (s + 1 - 2 * lax.rem(s, 2), f)


def seq_node(dp, dq):
    s, f = place()
    node = 2 * lax.rem(s // 4 + dp + 4, 4) + lax.rem(s // 2 + dq, 2)
    s_there = 2 * node + lax.rem(s, 2)
    return (s_there, f), s_there * SH


def fsdp_node(dp, dq):
    s, f = place()
    return (s, 2 * lax.rem(f // 2 + dp + 4, 4) + lax.rem(f + dq, 2))


def pair_of(device, sign):
    s, f = device
    x = lax.rem(s // 4 + sign * (f // 2) + 4, 4)
    return 2 * x + lax.rem(s // 2 + f + f // 2, 2)


def by_frames(dp, dq):
    device = fsdp_node(dp, dq)
    return device, pair_of(device, -1) * OWN


def by_positions(dp, dq):
    device = fsdp_node(dp, dq)
    return device, pair_of(device, 1) * OWN


def swap_out():
    s, f = place()
    return [(2 * pair_of((s, f), 1) + e, f) for e in range(2)]


def swap_back():
    s, f = place()
    return [(2 * pair_of((s, f), -1) + i, f) for i in range(2)]


def is_me(device):
    s, f = place()
    return jnp.logical_and(device[0] == s, device[1] == f)


def greet():
    barrier = pltpu.get_barrier_semaphore()
    peers = [sibling()]
    for dp, dq in ((1, 0), (-1, 0), (0, 1)):
        peers += [seq_node(dp, dq)[0], fsdp_node(dp, dq)]
    for peer in peers:
        pl.semaphore_signal(barrier, inc=1, device_id=peer, device_id_type=MESH)
    count = len(peers)
    for peer in swap_out() + swap_back():
        other = jnp.logical_not(is_me(peer))
        count = count + other.astype(jnp.int32)

        @pl.when(other)
        def _():
            pl.semaphore_signal(barrier, inc=1, device_id=peer, device_id_type=MESH)

    pl.semaphore_wait(barrier, count)


def rows_at(start, n):
    return pl.ds(pl.multiple_of(start, 16), n)


class Gather:
    NEAR = (
        ((0, 0), None, (1, 0)),
        ((0, 0), None, (-1, 0)),
        ((0, 0), None, (0, 1)),
        ((-1, 0), 0, (1, 0)),
        ((1, 0), 1, (-1, 0)),
        ((0, 1), None, (1, 0)),
        ((0, 1), None, (-1, 0)),
    )
    WIDE = (((2, 0), 0, (0, 1)), ((2, 0), 1, (0, 1)))
    SLIM = (((-1, 1), 0, (1, 0)), ((1, 1), 1, (-1, 0)))

    def __init__(self, ref, node, size, cols, sems, wide=True):
        self.ref, self.node, self.size, self.cols, self.sems, self.wide = ref, node, size, cols, sems, wide
        self.messages = self.NEAR + (self.WIDE if wide else self.SLIM)

    def copy(self, m):
        shard, half, target = self.messages[m]
        start, n = self.node(*shard)[1], self.size
        if half is not None:
            n = n // 2
            start = start + half * n
        rows = self.ref.at[rows_at(start, n), pl.ds(*self.cols)]
        return remote(rows, rows, self.sems.at[0, m], self.sems.at[1, m], self.node(*target)[0])

    def send(self, *messages):
        for m in messages:
            self.copy(m).start()

    def got(self, *messages):
        for m in messages:
            self.copy(m).wait_recv()

    def pass_on(self, *shards):
        pass

    def start(self):
        self.send(0, 1, 2)
        self.pass_on(0)

    def middle(self):
        self.got(0)
        self.send(3)
        self.pass_on(1)
        self.got(1)
        self.send(4)
        self.pass_on(2)
        self.got(2)
        self.send(5, 6)
        self.pass_on(3)

    def last(self):
        if self.wide:
            self.got(3)
            self.send(7)
            self.got(4)
            self.send(8)
            self.pass_on(4)
        else:
            self.got(5)
            self.send(7)
            self.pass_on(5)
            self.got(6)
            self.send(8)
            self.pass_on(6)

    def fifth(self):
        if self.wide:
            self.got(5)
            self.pass_on(5)
            self.got(6)
            self.pass_on(6)
        else:
            self.got(3, 4)
            self.pass_on(4)

    def end(self):
        self.got(7, 8)
        self.pass_on(7)

    def sent(self):
        for m in range(9):
            self.copy(m).wait_send()


class Weights(Gather):
    SHARDS = ((0, 0), (-1, 0), (1, 0), (0, 1), (2, 0), (-1, 1), (1, 1), (2, 1))

    def __init__(self, parts, w_ref, cols, sems, near_sems, local, wide):
        super().__init__(w_ref, seq_node, SH, cols, sems, wide)
        self.near_sems = near_sems
        rows = rows_at(seq_node(0, 0)[1], SH)
        self.own = [
            pltpu.make_async_copy(src, w_ref.at[rows, pl.ds(*at)], local.at[i]) for i, (src, at) in enumerate(parts)
        ]

    def near(self, n):
        rows = self.ref.at[rows_at(self.node(*self.SHARDS[n])[1], SH), pl.ds(*self.cols)]
        return remote(rows, rows, self.near_sems.at[0, n], self.near_sems.at[1, n], sibling())

    def near_got(self, *shards):
        for n in shards:
            self.near(n).wait_recv()

    def pass_on(self, *shards):
        for n in shards:
            self.near(n).start()

    def load(self):
        for copy in self.own:
            copy.start()

    def start(self):
        for copy in self.own:
            copy.wait()
        super().start()

    def sent(self):
        super().sent()
        for n in range(8):
            self.near(n).wait_send()


def add_rows(ref, start, n, cols, stage, base):
    at = pl.ds(*cols)

    @pl.loop(0, n // 16)
    def _(i):
        rows, here = rows_at(start + i * 16, 16), rows_at(base + i * 16, 16)
        ref[rows, at] = (ref[rows, at].astype(F32) + stage[here, at].astype(F32)).astype(BF16)


class Reduce:
    NEAR = (
        ((-1, 0), None, (-1, 0), 5),
        ((1, 0), None, (1, 0), 6),
        ((0, 1), None, (0, 1), 4),
        ((2, 0), 0, (-1, 0), 3),
        ((2, 0), 1, (1, 0), 3),
        ((-1, 1), None, (-1, 0), 1),
        ((1, 1), None, (1, 0), 2),
    )
    WIDE = (((2, 1), None, (0, 1), 0),)
    SLIM = (((2, 1), 0, (-1, 0), 0), ((2, 1), 1, (1, 0), 0))

    def __init__(self, ref, node, size, cols, held, sems, wide=True):
        self.ref, self.node, self.size, self.cols, self.held, self.sems = ref, node, size, cols, held, sems
        self.wide = wide
        self.messages = self.NEAR + (self.WIDE if wide else self.SLIM)

    def copy(self, m):
        shard, half, target, slot = self.messages[m]
        start, n, first = self.node(*shard)[1], self.size, 0
        if half is not None:
            n = n // 2
            first = half * n
        src = self.ref.at[rows_at(start + first, n), pl.ds(*self.cols)]
        dst = self.held.at[pl.ds(slot * self.size + first, n), pl.ds(*self.cols)]
        return remote(src, dst, self.sems.at[0, m], self.sems.at[1, m], self.node(*target)[0])

    def send(self, *messages):
        for m in messages:
            self.copy(m).start()

    def got(self, *messages):
        for m in messages:
            self.copy(m).wait_recv()

    def add(self, shard, slot, half=None):
        start, n, first = self.node(*shard)[1], self.size, 0
        if half is not None:
            n = n // 2
            first = half * n
        add_rows(self.ref, start + first, n, self.cols, self.held, slot * self.size + first)

    def ready(self, *shards):
        pass

    def start(self):
        if self.wide:
            self.ready((2, 1), (-1, 1), (1, 1))
            self.send(7, 5, 6)
        else:
            self.ready((2, 1))
            self.send(7, 8)
            self.ready((2, 0))
            self.send(3, 4)

    def middle(self):
        if self.wide:
            self.ready((2, 0))
            self.got(7)
            self.add((2, 0), 0)
            self.send(3, 4)
            self.ready((0, 1))
            self.got(5)
            self.add((0, 1), 1)
            self.got(6)
            self.add((0, 1), 2)
            self.send(2)
        else:
            self.ready((-1, 1))
            self.got(7)
            self.add((-1, 1), 0, 0)
            self.send(5)
            self.ready((1, 1))
            self.got(8)
            self.add((1, 1), 0, 1)
            self.send(6)
            self.nearest()

    def nearest(self):
        self.ready((-1, 0))
        self.got(3)
        self.add((-1, 0), 3, 0)
        self.send(0)
        self.ready((1, 0))
        self.got(4)
        self.add((1, 0), 3, 1)
        self.send(1)

    def last(self):
        if self.wide:
            self.nearest()
        else:
            self.ready((0, 1))
            self.got(5)
            self.add((0, 1), 1)
            self.got(6)
            self.add((0, 1), 2)
            self.send(2)

    def end(self):
        self.ready((0, 0))
        self.got(0, 1, 2)
        for m in range(len(self.messages)):
            self.copy(m).wait_send()

    def total(self, at):
        summed = self.ref[rows_at(self.node(0, 0)[1], self.size), at].astype(F32)
        for slot in (4, 5, 6):
            summed = summed + self.held[pl.ds(slot * self.size, self.size), at].astype(F32)
        return summed


class WeightGrads(Reduce):
    SHARDS = ((2, 1), (2, 0), (-1, 1), (1, 1), (-1, 0), (1, 0), (0, 1), (0, 0))

    def __init__(self, ref, cols, held, sems, near_held, near_sems):
        super().__init__(ref, seq_node, SH, cols, held, sems, False)
        self.near_held, self.near_sems = near_held, near_sems

    def near(self, n):
        s, _ = place()
        start = self.node(*self.SHARDS[n])[1] + (1 - 2 * lax.rem(s, 2)) * SH
        return remote(
            self.ref.at[rows_at(start, SH), pl.ds(*self.cols)],
            self.near_held.at[pl.ds(n * SH, SH), pl.ds(*self.cols)],
            self.near_sems.at[0, n], self.near_sems.at[1, n], sibling(),
        )

    def ready(self, *shards):
        for shard in shards:
            n = self.SHARDS.index(shard)
            self.near(n).wait_recv()
            add_rows(self.ref, self.node(*shard)[1], SH, self.cols, self.near_held, n * SH)

    def pair(self):
        for n in range(8):
            self.near(n).start()

    def result(self, block, gproj_ref, goutw_ref):
        base = self.node(0, 0)[1]
        at = pl.ds(*self.cols)

        @pl.loop(0, SH // 16)
        def _(i):
            rows, here = rows_at(base + i * 16, 16), rows_at(i * 16, 16)
            total = self.ref[rows, at].astype(F32)
            for slot in (4, 5, 6):
                total = total + self.held[rows_at(slot * SH + i * 16, 16), at].astype(F32)
            if self.cols[0] < PC:
                gproj_ref[block, here, at] = total.astype(BF16)
            else:
                goutw_ref[block, here, :] = total.astype(BF16)

        for n in range(8):
            self.near(n).wait_send()


class Parts:
    def __init__(self, *parts):
        self.parts = parts

    def __getattr__(self, step):
        def run(*args):
            for part in self.parts:
                getattr(part, step)(*args)

        return run


class Swap:
    def __init__(self, src_ref, dst_ref, cols, targets, base, sems, local):
        self.src_ref, self.dst_ref, self.targets, self.base = src_ref, dst_ref, targets, base
        self.cols, self.sems, self.local = pl.ds(*cols), sems, local

    def each(self, act):
        s, _ = place()
        for j in range(2):
            src = self.src_ref.at[pl.ds(j * 16, 16), self.cols]
            there = self.dst_ref.at[rows_at(s * 16, 16), self.cols]
            here = self.dst_ref.at[rows_at(self.base + j * 16, 16), self.cols]
            act(j, src, there, here)

    def start(self):
        s, _ = place()

        def act(j, src, there, here):
            mine = is_me(self.targets[j])

            @pl.when(mine)
            def _():
                pltpu.make_async_copy(src, here, self.local).start()

            @pl.when(jnp.logical_not(mine))
            def _():
                remote(src, there, self.sems.at[0, j], self.sems.at[1, lax.rem(s, 2)], self.targets[j]).start()

        self.each(act)

    def wait(self):
        def act(j, src, there, here):
            mine = is_me(self.targets[j])
            copy = lambda: remote(src, here, self.sems.at[0, j], self.sems.at[1, j], self.targets[j])

            @pl.when(mine)
            def _():
                pltpu.make_async_copy(src, here, self.local).wait()

            @pl.when(jnp.logical_not(mine))
            def _():
                copy().wait_send()
                copy().wait_recv()

        self.each(act)


def branch_end(x_ref, x_base, gate, reduced, out_ref, cols):
    @pl.loop(cols[0] // TILE, sum(cols) // TILE)
    def _(i):
        at = tile_at(i)
        value = x_ref[rows_at(x_base, OWN), at].astype(F32) + gate[:, at] * reduced.total(at)
        out_ref[:, at] = value.astype(BF16)


def input_grad(x_ref, x_base, dy_ref, dy_base, gain, reduced, sum_ref, out_ref):
    def moments(i, carry):
        squares, cross = carry
        at = tile_at(i)
        x = x_ref[rows_at(x_base, OWN), at].astype(F32)
        weighted = reduced.total(at) * gain[:, at]
        sum_ref[:, at] = weighted
        return squares + jnp.sum(x * x, -1, keepdims=True), cross + jnp.sum(x * weighted, -1, keepdims=True)

    zero = jnp.zeros((OWN, 1), F32)
    squares, cross = lax.fori_loop(0, NT, moments, (zero, zero))
    inverse = lax.rsqrt(squares / D + EPS)
    factor = inverse * inverse * inverse * (cross / D)

    @pl.loop(0, NT)
    def _(i):
        at = tile_at(i)
        x = x_ref[rows_at(x_base, OWN), at].astype(F32)
        value = dy_ref[rows_at(dy_base, OWN), at].astype(F32) + (inverse * sum_ref[:, at] - x * factor)
        out_ref[:, at] = value.astype(BF16)


def whole(
    x_ref, dy_ref, proj_in, outw_in, gain_ref, gate_ref, qkg_ref,
    mixed_ref, clip_ref, gproj_ref, goutw_ref,
    w0_ref, w1_ref, g_ref, normed0_ref, normed1_ref, proj0_ref, proj1_ref, att0_ref, att1_ref, datt_ref, dproj_ref,
    part_ref, part1_ref, middle_ref, grad_ref, held_ref, own_ref, sum_ref, near1_ref, far1_ref,
    w_sems, wn_sems, local, rs_sems, ag_sems, g_sems, gn_sems, swap_sems,
):
    s, f = place()
    x_group = s // 4
    gain0, gain1, gate0, gate1 = (r.at[pl.ds(b, 1)] for r in (gain_ref, gate_ref) for b in range(2))
    qkg0, qkg1 = qkg_ref[0], qkg_ref[1]
    proj_cols, outw_cols = (0, PC), (PC, WC - PC)
    w0p = Weights(
        [(proj_in.at[0], proj_cols)], w0_ref, proj_cols, w_sems.at[0], wn_sems.at[0], local.at[0], True
    )
    w0o = Weights(
        [(outw_in.at[0], outw_cols)], w0_ref, outw_cols, w_sems.at[1], wn_sems.at[1], local.at[1], True
    )
    w1 = [
        Weights([(src, cols)], w1_ref, cols, w_sems.at[2 + i], wn_sems.at[2 + i], local.at[2 + i], False)
        for i, (src, cols) in enumerate(
            (
                (proj_in.at[1, :, pl.ds(0, 384)], (0, 384)),
                (proj_in.at[1, :, pl.ds(384, 384)], (384, 384)),
                (outw_in.at[1], outw_cols),
            )
        )
    ]
    positions, frames = by_positions(0, 0)[1], by_frames(0, 0)[1]
    whole_rows, halves = (0, D), ((0, 2048), (2048, 1536))
    shards = range(8)

    def two(make, *args):
        return Parts(*(make(cols, i, *args) for i, cols in enumerate(halves)))

    def reduce_of(cols, i, node, held, first_sem):
        return Reduce(part_ref, node, OWN, cols, held_ref.at[held], rs_sems.at[first_sem + i])

    def gather_of(cols, i, ref, node, first_sem):
        return Gather(ref, node, OWN, cols, ag_sems.at[first_sem + i])

    w0p.load()
    w0o.load()
    for weights in w1:
        weights.load()
    greet()
    w0p.start()
    normalise(x_ref, gain0, normed0_ref)
    w0o.start()
    w0p.middle()
    w0o.middle()
    w0p.near_got(0, 3)
    project(x_group, normed0_ref, w0_ref, proj0_ref, True)
    w0p.last()
    w0p.fifth()
    w0p.near_got(1, 5)
    project(lax.rem(x_group + 3, 4), normed0_ref, w0_ref, proj0_ref, False)
    w0p.near_got(2, 6)
    project(lax.rem(x_group + 1, 4), normed0_ref, w0_ref, proj0_ref, False)
    w0o.last()
    w0p.end()
    w0p.near_got(4, 7)
    w1[0].start()
    project(lax.rem(x_group + 2, 4), normed0_ref, w0_ref, proj0_ref, False)
    attend(proj0_ref, qkg0, att0_ref, False)
    w0o.fifth()
    w0o.end()
    w0o.near_got(*shards)

    r0 = two(reduce_of, by_positions, 0, 0)
    for piece, cols in zip(r0.parts, halves):
        branch(att0_ref, w0_ref, part_ref, cols)
        piece.start()
    w1[0].middle()
    w1[1].start()
    r0.middle()
    w1[0].last()
    r0.last()
    swaps = []
    for i, cols in enumerate(halves):
        r0.parts[i].end()
        branch_end(x_ref, positions, gate0, r0.parts[i], own_ref.at[0], cols)
        swaps.append(
            Swap(own_ref.at[0], middle_ref, cols, swap_out(), frames, swap_sems.at[i], local.at[5, i])
        )
        swaps[i].start()
        if i == 0:
            w1[1].middle()
    a0 = two(gather_of, middle_ref, by_frames, 0)
    for i in range(2):
        swaps[i].wait()
        a0.parts[i].start()
    w1[1].last()
    w1[2].start()
    w1[0].fifth()
    w1[0].end()
    a0.middle()
    w1[2].middle()
    w1[1].fifth()
    w1[1].end()
    a0.last()
    w1[2].last()
    w1[2].fifth()
    w1[2].end()
    for weights in (w0p, w0o, *w1):
        weights.sent()
    for weights in w1:
        weights.near_got(*shards)
    attended_grad(dy_ref, w1_ref, gate1, datt_ref)
    a0.fifth()
    a0.end()
    a0.sent()

    normalise(middle_ref, gain1, normed1_ref)
    for group in range(4):
        project(group, normed1_ref, w1_ref, proj1_ref, group == 0)
    attend(proj1_ref, qkg1, att1_ref, True)
    branch(att1_ref, w1_ref, part1_ref, whole_rows)
    r1 = Reduce(part1_ref, by_frames, OWN, whole_rows, held_ref.at[1], rs_sems.at[2])
    r1.start()
    grad_cols = ((PC, WC - PC), (0, 384), (384, 384))
    grads1 = [
        WeightGrads(g_ref, cols, far1_ref, g_sems.at[i], near1_ref, gn_sems.at[i]) for i, cols in enumerate(grad_cols)
    ]
    outw_grads(dy_ref, gate1, att1_ref, g_ref)
    grads1[0].pair()
    projected_grad(qkg1, proj1_ref, datt_ref, dproj_ref, True)

    r2 = two(reduce_of, by_frames, 2, 3)
    for piece, cols in zip(r2.parts, halves):
        normed_grad(dproj_ref, w1_ref, part_ref, cols)
        piece.start()
    grads1[0].start()
    for i in (1, 2):
        proj_grads(normed1_ref, dproj_ref, g_ref, grad_cols[i])
        grads1[i].pair()
    r2.middle()
    grads1[1].start()
    r1.middle()
    r2.last()
    grads1[0].middle()
    r2.end()
    input_grad(middle_ref, frames, dy_ref, frames, gain1, r2.parts[0], sum_ref, own_ref.at[1])
    a1 = two(gather_of, grad_ref, by_positions, 2)
    swaps = [
        Swap(own_ref.at[1], grad_ref, cols, swap_back(), positions, swap_sems.at[2 + i], local.at[5, i])
        for i, cols in enumerate(halves)
    ]
    for i in range(2):
        swaps[i].start()
    r1.last()
    grads1[0].last()
    for i in range(2):
        swaps[i].wait()
        a1.parts[i].start()
    grads1[1].middle()
    a1.middle()
    grads1[2].start()
    a1.last()
    grads1[1].last()
    r1.end()
    branch_end(middle_ref, frames, gate1, r1, own_ref.at[2], whole_rows)
    keep = pltpu.make_async_copy(own_ref.at[2], mixed_ref.at[rows_at(frames, OWN)], local.at[6, 0])
    keep.start()
    keep.wait()
    a1.fifth()
    a2 = Gather(mixed_ref, by_frames, OWN, whole_rows, ag_sems.at[4])
    a2.start()
    grads1[2].middle()
    a1.end()

    attended_grad(grad_ref, w0_ref, gate0, datt_ref)
    projected_grad(qkg0, proj0_ref, datt_ref, dproj_ref, False)
    r3 = two(reduce_of, by_positions, 3, 5)
    for piece, cols in zip(r3.parts, halves):
        normed_grad(dproj_ref, w0_ref, part_ref, cols)
        piece.start()
    near0_ref, far0_ref = w1_ref.at[pl.ds(0, 8 * SH)], w1_ref.at[pl.ds(8 * SH, 7 * SH)]
    grads0 = [
        WeightGrads(w0_ref, cols, far0_ref, g_sems.at[3 + i], near0_ref, gn_sems.at[3 + i])
        for i, cols in enumerate(grad_cols)
    ]
    proj_grads(normed0_ref, dproj_ref, w0_ref, grad_cols[1])
    grads0[1].pair()
    a2.middle()
    proj_grads(normed0_ref, dproj_ref, w0_ref, grad_cols[2])
    grads0[2].pair()
    r3.middle()
    grads0[1].start()
    outw_grads(grad_ref, gate0, att0_ref, w0_ref)
    grads0[0].pair()
    r3.last()
    grads0[2].start()
    grads1[2].last()
    grads0[1].middle()
    r3.end()
    input_grad(x_ref, positions, grad_ref, positions, gain0, r3.parts[0], sum_ref, own_ref.at[3])
    keep = pltpu.make_async_copy(own_ref.at[3], clip_ref.at[rows_at(positions, OWN)], local.at[6, 1])
    keep.start()
    grads0[0].start()
    keep.wait()
    a3 = two(gather_of, clip_ref, by_positions, 5)
    a3.start()
    a2.last()
    grads0[2].middle()
    grads0[0].middle()
    a3.middle()
    grads0[1].last()
    a3.last()
    grads0[2].last()
    for i in range(3):
        grads1[i].end()
        grads1[i].result(1, gproj_ref, goutw_ref)
    grads0[0].last()
    a1.sent()
    a2.fifth()
    a2.end()
    a2.sent()
    a3.fifth()
    for i in (1, 2, 0):
        grads0[i].end()
        grads0[i].result(0, gproj_ref, goutw_ref)
    a3.end()
    a3.sent()


def shaped(shape, dtype=BF16):
    return jax.ShapeDtypeStruct(shape, dtype)


def sem(*shape):
    return pltpu.SemaphoreType.DMA(shape)


def local_program(clip_tokens, out_cotangent, proj_weight, out_weight, norm_gain, branch_gate, qk_gain):
    in_vmem = pl.BlockSpec(memory_space=pltpu.VMEM)
    anywhere = pl.BlockSpec(memory_space=pl.ANY)
    tokens = lambda *lead: pltpu.VMEM((*lead, T, D), BF16)
    mixed, clip, gproj, goutw = pl.pallas_call(
        whole,
        out_shape=[shaped((T, D)), shaped((T, D)), shaped((2, SH, PC)), shaped((2, SH, WC - PC))],
        in_specs=[in_vmem, in_vmem, anywhere, anywhere, in_vmem, in_vmem, in_vmem],
        out_specs=[anywhere, anywhere, in_vmem, in_vmem],
        scratch_shapes=[
            pltpu.VMEM((D, WC), BF16),
            pltpu.VMEM((D, WC), BF16),
            pltpu.VMEM((D, WC), BF16),
            tokens(),
            tokens(),
            pltpu.VMEM((T, PC), F32),
            pltpu.VMEM((T, PC), F32),
            pltpu.VMEM((T, 2 * HD), BF16),
            pltpu.VMEM((T, 2 * HD), BF16),
            pltpu.VMEM((T, 2 * HD), F32),
            pltpu.VMEM((T, PC), BF16),
            tokens(),
            tokens(),
            tokens(),
            tokens(),
            pltpu.VMEM((4, 7 * OWN, D), BF16),
            pltpu.VMEM((4, OWN, D), BF16),
            pltpu.VMEM((OWN, D), F32),
            pltpu.VMEM((8 * SH, WC), BF16),
            pltpu.VMEM((7 * SH, WC), BF16),
            sem(5, 2, 9),
            sem(5, 2, 8),
            sem(7, 2),
            sem(7, 2, 9),
            sem(7, 2, 9),
            sem(6, 2, 9),
            sem(6, 2, 8),
            sem(4, 2, 2),
        ],
        compiler_params=pltpu.CompilerParams(
            vmem_limit_bytes=VMEM_LIMIT, collective_id=0, has_side_effects=True
        ),
        name="two_blocks",
    )(
        clip_tokens.reshape(T, D),
        out_cotangent.reshape(T, D),
        proj_weight,
        jnp.swapaxes(out_weight, 1, 2),
        norm_gain,
        branch_gate,
        qk_gain,
    )
    return mixed.reshape(16, 16, D), clip.reshape(1, T, D), gproj, jnp.swapaxes(goutw, 1, 2)


def solution(mesh):
    placed = (
        P("seq", None, None),
        P(None, "seq", None),
        P(None, "seq", "fsdp"),
        P(None, "fsdp", "seq"),
        P(),
        P(),
        P(),
    )
    return jax.shard_map(
        local_program,
        mesh=mesh,
        in_specs=placed,
        out_specs=(
            P(None, "seq", None),
            P("seq", None, None),
            P(None, "seq", "fsdp"),
            P(None, "fsdp", "seq"),
        ),
        check_vma=False,
    )
```

```python
import functools

import jax
import jax.numpy as jnp
from jax import lax
from jax.experimental import pallas as pl
from jax.experimental.pallas import tpu as pltpu
from jax.sharding import PartitionSpec as P

EPS = 1e-06
MESH = pl.DeviceIdType.MESH
D = 3584
HD = 128
T = 256
OWN = 32
GROUP = 896
SH = 224
WC = 1024
PC = 768
TILE = 512
NT = D // TILE
PART = 896
F32 = jnp.float32
BF16 = jnp.bfloat16
VMEM_LIMIT = 55 * 1024 * 1024


def tile_at(i, size=TILE):
    return pl.ds(pl.multiple_of(i * size, size), size)


def dot(a, b, contract=((1,), (0,))):
    return lax.dot_general(a, b, (contract, ((), ())), preferred_element_type=F32)


def head_forward(proj_ref, qkg, head, temporal):
    base = head * 3 * HD
    q_raw = proj_ref[:, base : base + HD]
    k_raw = proj_ref[:, base + HD : base + 2 * HD]
    q_inv = lax.rsqrt(jnp.mean(q_raw * q_raw, -1, keepdims=True) + EPS)
    k_inv = lax.rsqrt(jnp.mean(k_raw * k_raw, -1, keepdims=True) + EPS)
    q = (q_raw * q_inv * qkg[0:1, :]).astype(BF16)
    k = (k_raw * k_inv * qkg[1:2, :]).astype(BF16)
    v = proj_ref[:, base + 2 * HD : base + 3 * HD].astype(BF16)
    scores = dot(q, k, ((1,), (1,))) * HD**-0.5
    if temporal:
        rows = lax.broadcasted_iota(jnp.int32, (T, T), 0)
        cols = lax.broadcasted_iota(jnp.int32, (T, T), 1)
        scores = jnp.where((rows & 15) == (cols & 15), scores, -1e30)
    top = jnp.max(scores, -1, keepdims=True)
    grown = jnp.exp(scores - top)
    probs = grown / jnp.sum(grown, -1, keepdims=True)
    return q_raw, k_raw, q_inv, k_inv, q, k, v, probs


def head_backward(proj_ref, qkg, head, temporal, d_att, dproj_ref):
    q_raw, k_raw, q_inv, k_inv, q, k, v, probs = head_forward(proj_ref, qkg, head, temporal)
    base = head * 3 * HD
    rounded = probs.astype(BF16)
    d_probs = dot(d_att, v, ((1,), (1,))).astype(BF16).astype(F32)
    d_v = dot(rounded, d_att, ((0,), (0,)))
    d_scores = probs * (d_probs - jnp.sum(probs * d_probs, -1, keepdims=True))
    d_scores = (d_scores * HD**-0.5).astype(BF16)
    d_q = dot(d_scores, k).astype(BF16).astype(F32) * qkg[0:1, :]
    d_k = dot(d_scores, q, ((0,), (0,))).astype(BF16).astype(F32) * qkg[1:2, :]
    d_q = q_inv * d_q - q_raw * (q_inv * q_inv * q_inv) * jnp.mean(q_raw * d_q, -1, keepdims=True)
    d_k = k_inv * d_k - k_raw * (k_inv * k_inv * k_inv) * jnp.mean(k_raw * d_k, -1, keepdims=True)
    dproj_ref[:, base : base + HD] = d_q.astype(BF16)
    dproj_ref[:, base + HD : base + 2 * HD] = d_k.astype(BF16)
    dproj_ref[:, base + 2 * HD : base + 3 * HD] = d_v.astype(BF16)


def inverse_norm(x_ref):
    def square(i, total):
        x = x_ref[:, tile_at(i)].astype(F32)
        return total + jnp.sum(x * x, -1, keepdims=True)

    total = lax.fori_loop(0, NT, square, jnp.zeros((T, 1), F32))
    return lax.rsqrt(total / D + EPS)


def normalise(x_ref, gain, normed_ref):
    inverse = inverse_norm(x_ref)

    @pl.loop(0, NT)
    def _(i):
        at = tile_at(i)
        normed_ref[:, at] = (x_ref[:, at].astype(F32) * inverse * gain[:, at]).astype(BF16)


def project_scaled(x_ref, w_ref, gain, proj_ref, cols, squares):
    def step(i, squares):
        at = tile_at(i, PART)
        x = x_ref[:, at].astype(F32)
        proj_ref[...] += dot((x * gain[:, at]).astype(BF16), w_ref[at, :PC])
        return squares + jnp.sum(x * x, -1, keepdims=True)

    return lax.fori_loop(cols[0] // PART, sum(cols) // PART, step, squares)


def project(group, normed_ref, w_ref, proj_ref, first):
    at = tile_at(group, GROUP)
    product = dot(normed_ref[:, at], w_ref[at, :PC])
    if first:
        proj_ref[...] = product
    else:
        proj_ref[...] += product


def attend(proj_ref, qkg, att_ref, temporal):
    for head in range(2):
        parts = head_forward(proj_ref, qkg, head, temporal)
        att_ref[:, head * HD : (head + 1) * HD] = dot(parts[7].astype(BF16), parts[6]).astype(BF16)


def branch(att_ref, w_ref, part_ref, cols):
    att = att_ref[...]

    @pl.loop(cols[0] // PART, sum(cols) // PART)
    def _(i):
        at = tile_at(i, PART)
        part_ref[:, at] = dot(att, w_ref[at, PC:], ((1,), (1,))).astype(BF16)


def scaled_tile(dy_ref, gate, at):
    return (dy_ref[:, at].astype(F32) * gate[:, at]).astype(BF16)


def attended_grad(dy_ref, w_ref, gate, datt_ref, cols):
    if cols[0] == 0:
        datt_ref[...] = jnp.zeros_like(datt_ref)

    @pl.loop(cols[0] // PART, sum(cols) // PART)
    def _(i):
        at = tile_at(i, PART)
        datt_ref[...] += dot(scaled_tile(dy_ref, gate, at), w_ref[at, PC:])


def projected_grad(qkg, proj_ref, datt_ref, dproj_ref, temporal):
    for head in range(2):
        d_att = datt_ref[:, head * HD : (head + 1) * HD].astype(BF16)
        head_backward(proj_ref, qkg, head, temporal, d_att, dproj_ref)


def normed_grad(dproj_ref, w_ref, dpart_ref, cols):
    dproj = dproj_ref[...]

    @pl.loop(cols[0] // PART, sum(cols) // PART)
    def _(i):
        at = tile_at(i, PART)
        dpart_ref[:, at] = dot(dproj, w_ref[at, :PC], ((1,), (1,))).astype(BF16)


def proj_grads(normed_ref, dproj_ref, g_ref, cols):
    to = pl.ds(*cols)
    dproj = dproj_ref[:, to]

    @pl.loop(0, NT)
    def _(i):
        at = tile_at(i)
        g_ref[at, to] = dot(normed_ref[:, at], dproj, ((0,), (0,))).astype(BF16)


def outw_grads(dy_ref, gate, att_ref, g_ref, cols):
    att = att_ref[...]

    @pl.loop(cols[0] // PART, sum(cols) // PART)
    def _(i):
        at = tile_at(i, PART)
        g_ref[at, PC:] = dot(scaled_tile(dy_ref, gate, at), att, ((0,), (0,))).astype(BF16)


def place():
    return lax.axis_index("seq"), lax.axis_index("fsdp")


def remote(src, dst, send, recv, device):
    return pltpu.make_async_remote_copy(
        src_ref=src, dst_ref=dst, send_sem=send, recv_sem=recv, device_id=device, device_id_type=MESH
    )


def sibling():
    s, f = place()
    return (s + 1 - 2 * lax.rem(s, 2), f)


def seq_node(dp, dq):
    s, f = place()
    node = 2 * lax.rem(s // 4 + dp + 4, 4) + lax.rem(s // 2 + dq, 2)
    s_there = 2 * node + lax.rem(s, 2)
    return (s_there, f), s_there * SH


def fsdp_node(dp, dq):
    s, f = place()
    return (s, 2 * lax.rem(f // 2 + dp + 4, 4) + lax.rem(f + dq, 2))


def pair_of(device, sign):
    s, f = device
    x = lax.rem(s // 4 + sign * (f // 2) + 4, 4)
    return 2 * x + lax.rem(s // 2 + f + f // 2, 2)


def by_frames(dp, dq):
    device = fsdp_node(dp, dq)
    return device, pair_of(device, -1) * OWN


def by_positions(dp, dq):
    device = fsdp_node(dp, dq)
    return device, pair_of(device, 1) * OWN


def swap_out():
    s, f = place()
    return [(2 * pair_of((s, f), 1) + e, f) for e in range(2)]


def swap_back():
    s, f = place()
    return [(2 * pair_of((s, f), -1) + i, f) for i in range(2)]


def is_me(device):
    s, f = place()
    return jnp.logical_and(device[0] == s, device[1] == f)


def greet():
    barrier = pltpu.get_barrier_semaphore()
    peers = [sibling()]
    for dp, dq in ((1, 0), (-1, 0), (0, 1)):
        peers += [seq_node(dp, dq)[0], fsdp_node(dp, dq)]
    for peer in peers:
        pl.semaphore_signal(barrier, inc=1, device_id=peer, device_id_type=MESH)
    count = len(peers)
    for peer in swap_out() + swap_back():
        other = jnp.logical_not(is_me(peer))
        count = count + other.astype(jnp.int32)

        @pl.when(other)
        def _():
            pl.semaphore_signal(barrier, inc=1, device_id=peer, device_id_type=MESH)

    pl.semaphore_wait(barrier, count)


def rows_at(start, n):
    return pl.ds(pl.multiple_of(start, 16), n)


class Gather:
    NEAR = (
        ((0, 0), None, (1, 0)),
        ((0, 0), None, (-1, 0)),
        ((0, 0), None, (0, 1)),
        ((-1, 0), 0, (1, 0)),
        ((1, 0), 1, (-1, 0)),
        ((0, 1), None, (1, 0)),
        ((0, 1), None, (-1, 0)),
    )
    WIDE = (((2, 0), 0, (0, 1)), ((2, 0), 1, (0, 1)))
    SLIM = (((-1, 1), 0, (1, 0)), ((1, 1), 1, (-1, 0)))

    def __init__(self, ref, node, size, cols, sems, wide=True):
        self.ref, self.node, self.size, self.cols, self.sems, self.wide = ref, node, size, cols, sems, wide
        self.messages = self.NEAR + (self.WIDE if wide else self.SLIM)

    def copy(self, m):
        shard, half, target = self.messages[m]
        start, n = self.node(*shard)[1], self.size
        if half is not None:
            n = n // 2
            start = start + half * n
        rows = self.ref.at[rows_at(start, n), pl.ds(*self.cols)]
        return remote(rows, rows, self.sems.at[0, m], self.sems.at[1, m], self.node(*target)[0])

    def send(self, *messages):
        for m in messages:
            self.copy(m).start()

    def got(self, *messages):
        for m in messages:
            self.copy(m).wait_recv()

    def pass_on(self, *shards):
        pass

    def start(self):
        self.send(0, 1, 2)
        self.pass_on(0)

    def middle(self):
        self.got(0)
        self.send(3)
        self.pass_on(1)
        self.got(1)
        self.send(4)
        self.pass_on(2)
        self.got(2)
        self.send(5, 6)
        self.pass_on(3)

    def last(self):
        if self.wide:
            self.got(3)
            self.send(7)
            self.got(4)
            self.send(8)
            self.pass_on(4)
        else:
            self.got(5)
            self.send(7)
            self.pass_on(5)
            self.got(6)
            self.send(8)
            self.pass_on(6)

    def fifth(self):
        if self.wide:
            self.got(5)
            self.pass_on(5)
            self.got(6)
            self.pass_on(6)
        else:
            self.got(3, 4)
            self.pass_on(4)

    def end(self):
        self.got(7, 8)
        self.pass_on(7)

    def sent(self):
        for m in range(9):
            self.copy(m).wait_send()


class Weights(Gather):
    SHARDS = ((0, 0), (-1, 0), (1, 0), (0, 1), (2, 0), (-1, 1), (1, 1), (2, 1))

    def __init__(self, parts, w_ref, cols, sems, near_sems, local, wide):
        super().__init__(w_ref, seq_node, SH, cols, sems, wide)
        self.near_sems = near_sems
        rows = rows_at(seq_node(0, 0)[1], SH)
        self.own = [
            pltpu.make_async_copy(src, w_ref.at[rows, pl.ds(*at)], local.at[i]) for i, (src, at) in enumerate(parts)
        ]

    def near(self, n):
        rows = self.ref.at[rows_at(self.node(*self.SHARDS[n])[1], SH), pl.ds(*self.cols)]
        return remote(rows, rows, self.near_sems.at[0, n], self.near_sems.at[1, n], sibling())

    def near_got(self, *shards):
        for n in shards:
            self.near(n).wait_recv()

    def pass_on(self, *shards):
        for n in shards:
            self.near(n).start()

    def load(self):
        for copy in self.own:
            copy.start()

    def start(self):
        for copy in self.own:
            copy.wait()
        super().start()

    def sent(self):
        super().sent()
        for n in range(8):
            self.near(n).wait_send()


def add_rows(ref, start, n, cols, stage, base):
    at = pl.ds(*cols)

    @pl.loop(0, n // 16)
    def _(i):
        rows, here = rows_at(start + i * 16, 16), rows_at(base + i * 16, 16)
        ref[rows, at] = (ref[rows, at].astype(F32) + stage[here, at].astype(F32)).astype(BF16)


class Reduce:
    NEAR = (
        ((-1, 0), None, (-1, 0), 5),
        ((1, 0), None, (1, 0), 6),
        ((0, 1), None, (0, 1), 4),
        ((2, 0), 0, (-1, 0), 3),
        ((2, 0), 1, (1, 0), 3),
        ((-1, 1), None, (-1, 0), 1),
        ((1, 1), None, (1, 0), 2),
    )
    WIDE = (((2, 1), None, (0, 1), 0),)
    SLIM = (((2, 1), 0, (-1, 0), 0), ((2, 1), 1, (1, 0), 0))

    def __init__(self, ref, node, size, cols, held, sems, wide=True):
        self.ref, self.node, self.size, self.cols, self.held, self.sems = ref, node, size, cols, held, sems
        self.wide = wide
        self.messages = self.NEAR + (self.WIDE if wide else self.SLIM)

    def copy(self, m):
        shard, half, target, slot = self.messages[m]
        start, n, first = self.node(*shard)[1], self.size, 0
        if half is not None:
            n = n // 2
            first = half * n
        src = self.ref.at[rows_at(start + first, n), pl.ds(*self.cols)]
        dst = self.held.at[pl.ds(slot * self.size + first, n), pl.ds(*self.cols)]
        return remote(src, dst, self.sems.at[0, m], self.sems.at[1, m], self.node(*target)[0])

    def send(self, *messages):
        for m in messages:
            self.copy(m).start()

    def got(self, *messages):
        for m in messages:
            self.copy(m).wait_recv()

    def add(self, shard, slot, half=None):
        start, n, first = self.node(*shard)[1], self.size, 0
        if half is not None:
            n = n // 2
            first = half * n
        add_rows(self.ref, start + first, n, self.cols, self.held, slot * self.size + first)

    def ready(self, *shards):
        pass

    def start(self):
        if self.wide:
            self.ready((2, 1), (-1, 1), (1, 1))
            self.send(7, 5, 6)
        else:
            self.ready((2, 1))
            self.send(7, 8)
            self.ready((2, 0))
            self.send(3, 4)

    def middle(self):
        if self.wide:
            self.ready((2, 0))
            self.got(7)
            self.add((2, 0), 0)
            self.send(3, 4)
            self.ready((0, 1))
            self.got(5)
            self.add((0, 1), 1)
            self.got(6)
            self.add((0, 1), 2)
            self.send(2)
        else:
            self.ready((-1, 1))
            self.got(7)
            self.add((-1, 1), 0, 0)
            self.send(5)
            self.ready((1, 1))
            self.got(8)
            self.add((1, 1), 0, 1)
            self.send(6)
            self.nearest()

    def nearest(self):
        self.ready((-1, 0))
        self.got(3)
        self.add((-1, 0), 3, 0)
        self.send(0)
        self.ready((1, 0))
        self.got(4)
        self.add((1, 0), 3, 1)
        self.send(1)

    def last(self):
        if self.wide:
            self.nearest()
        else:
            self.ready((0, 1))
            self.got(5)
            self.add((0, 1), 1)
            self.got(6)
            self.add((0, 1), 2)
            self.send(2)

    def end(self):
        self.ready((0, 0))
        self.got(0, 1, 2)
        for m in range(len(self.messages)):
            self.copy(m).wait_send()

    def total(self, at):
        summed = self.ref[rows_at(self.node(0, 0)[1], self.size), at].astype(F32)
        for slot in (4, 5, 6):
            summed = summed + self.held[pl.ds(slot * self.size, self.size), at].astype(F32)
        return summed


class WeightGrads(Reduce):
    SHARDS = ((2, 1), (2, 0), (-1, 1), (1, 1), (-1, 0), (1, 0), (0, 1), (0, 0))

    def __init__(self, ref, cols, held, sems, near_held, near_sems):
        super().__init__(ref, seq_node, SH, cols, held, sems, False)
        self.near_held, self.near_sems = near_held, near_sems

    def near(self, n):
        s, _ = place()
        start = self.node(*self.SHARDS[n])[1] + (1 - 2 * lax.rem(s, 2)) * SH
        return remote(
            self.ref.at[rows_at(start, SH), pl.ds(*self.cols)],
            self.near_held.at[pl.ds(n * SH, SH), pl.ds(*self.cols)],
            self.near_sems.at[0, n], self.near_sems.at[1, n], sibling(),
        )

    def ready(self, *shards):
        for shard in shards:
            n = self.SHARDS.index(shard)
            self.near(n).wait_recv()
            add_rows(self.ref, self.node(*shard)[1], SH, self.cols, self.near_held, n * SH)

    def pair(self):
        for n in range(8):
            self.near(n).start()

    def result(self, block, gproj_ref, goutw_ref):
        base = self.node(0, 0)[1]
        at = pl.ds(*self.cols)

        @pl.loop(0, SH // 16)
        def _(i):
            rows, here = rows_at(base + i * 16, 16), rows_at(i * 16, 16)
            total = self.ref[rows, at].astype(F32)
            for slot in (4, 5, 6):
                total = total + self.held[rows_at(slot * SH + i * 16, 16), at].astype(F32)
            if self.cols[0] < PC:
                gproj_ref[block, here, at] = total.astype(BF16)
            else:
                goutw_ref[block, here, :] = total.astype(BF16)

        for n in range(8):
            self.near(n).wait_send()


class Parts:
    def __init__(self, *parts):
        self.parts = parts

    def __getattr__(self, step):
        def run(*args):
            for part in self.parts:
                getattr(part, step)(*args)

        return run


class Swap:
    def __init__(self, src_ref, dst_ref, cols, targets, base, sems, local):
        self.src_ref, self.dst_ref, self.targets, self.base = src_ref, dst_ref, targets, base
        self.cols, self.sems, self.local = pl.ds(*cols), sems, local

    def each(self, act):
        s, _ = place()
        for j in range(2):
            src = self.src_ref.at[pl.ds(j * 16, 16), self.cols]
            there = self.dst_ref.at[rows_at(s * 16, 16), self.cols]
            here = self.dst_ref.at[rows_at(self.base + j * 16, 16), self.cols]
            act(j, src, there, here)

    def start(self):
        s, _ = place()

        def act(j, src, there, here):
            mine = is_me(self.targets[j])

            @pl.when(mine)
            def _():
                pltpu.make_async_copy(src, here, self.local).start()

            @pl.when(jnp.logical_not(mine))
            def _():
                remote(src, there, self.sems.at[0, j], self.sems.at[1, lax.rem(s, 2)], self.targets[j]).start()

        self.each(act)

    def wait(self):
        def act(j, src, there, here):
            mine = is_me(self.targets[j])
            copy = lambda: remote(src, here, self.sems.at[0, j], self.sems.at[1, j], self.targets[j])

            @pl.when(mine)
            def _():
                pltpu.make_async_copy(src, here, self.local).wait()

            @pl.when(jnp.logical_not(mine))
            def _():
                copy().wait_send()
                copy().wait_recv()

        self.each(act)


def branch_end(x_ref, x_base, gate, reduced, out_ref, base, cols):
    @pl.loop(cols[0] // PART, sum(cols) // PART)
    def _(i):
        at = tile_at(i, PART)
        value = x_ref[rows_at(x_base, OWN), at].astype(F32) + gate[:, at] * reduced.total(at)
        out_ref[rows_at(base, OWN), at] = value.astype(BF16)


def input_grad(x_ref, x_base, dy_ref, dy_base, gain, reduced, sum_ref, out_ref, base):
    def moments(i, carry):
        squares, cross = carry
        at = tile_at(i)
        x = x_ref[rows_at(x_base, OWN), at].astype(F32)
        weighted = reduced.total(at) * gain[:, at]
        sum_ref[:, at] = weighted
        return squares + jnp.sum(x * x, -1, keepdims=True), cross + jnp.sum(x * weighted, -1, keepdims=True)

    zero = jnp.zeros((OWN, 1), F32)
    squares, cross = lax.fori_loop(0, NT, moments, (zero, zero))
    inverse = lax.rsqrt(squares / D + EPS)
    factor = inverse * inverse * inverse * (cross / D)

    @pl.loop(0, NT)
    def _(i):
        at = tile_at(i)
        x = x_ref[rows_at(x_base, OWN), at].astype(F32)
        value = dy_ref[rows_at(dy_base, OWN), at].astype(F32) + (inverse * sum_ref[:, at] - x * factor)
        out_ref[rows_at(base, OWN), at] = value.astype(BF16)


def whole(
    x_in, dy_in, proj_in, outw_in, gain_ref, gate_ref, qkg_ref,
    mixed_ref, clip_ref, gproj_ref, goutw_ref,
    x_ref, dy_ref, w0_ref, w1_ref, g_ref, normed0_ref, normed1_ref, proj0_ref, proj1_ref, att0_ref, att1_ref, datt_ref, dproj_ref,
    part_ref, part1_ref, middle_ref, grad_ref, held_ref, own_ref, sum_ref, near1_ref, far1_ref,
    w_sems, wn_sems, local, rs_sems, ag_sems, g_sems, gn_sems, swap_sems,
):
    s, f = place()
    x_group = s // 4
    gain0, gain1, gate0, gate1 = (r.at[pl.ds(b, 1)] for r in (gain_ref, gate_ref) for b in range(2))
    qkg0, qkg1 = qkg_ref[0], qkg_ref[1]
    proj_cols, outw_cols = (0, PC), (PC, WC - PC)
    w0p = Weights(
        [(proj_in.at[0], proj_cols)], w0_ref, proj_cols, w_sems.at[0], wn_sems.at[0], local.at[0], True
    )
    w0o = Weights(
        [(outw_in.at[0], outw_cols)], w0_ref, outw_cols, w_sems.at[1], wn_sems.at[1], local.at[1], True
    )
    w1 = [
        Weights([(src, cols)], w1_ref, cols, w_sems.at[2 + i], wn_sems.at[2 + i], local.at[2 + i], False)
        for i, (src, cols) in enumerate(
            (
                (outw_in.at[1], outw_cols),
                (proj_in.at[1, :, pl.ds(0, 384)], (0, 384)),
                (proj_in.at[1, :, pl.ds(384, 384)], (384, 384)),
            )
        )
    ]
    positions, frames = by_positions(0, 0)[1], by_frames(0, 0)[1]
    whole_rows, halves = (0, D), [(0, 2 * PART), (2 * PART, 2 * PART)]
    shards = range(8)

    def parted(make, *args):
        return Parts(*(make(cols, i, *args) for i, cols in enumerate(halves)))

    def reduce_of(cols, i, node, held, first_sem):
        return Reduce(part_ref, node, OWN, cols, held_ref.at[held], rs_sems.at[first_sem + i])

    def gather_of(cols, i, ref, node, first_sem, wide=True):
        return Gather(ref, node, OWN, cols, ag_sems.at[first_sem + i], wide)

    w0p.load()
    w0o.load()
    for weights in w1:
        weights.load()
    x_load = pltpu.make_async_copy(x_in, x_ref, local.at[6, 0])
    dy_load = pltpu.make_async_copy(dy_in, dy_ref, local.at[6, 1])
    x_load.start()
    dy_load.start()
    greet()
    w0p.start()
    x_load.wait()
    normalise(x_ref, gain0, normed0_ref)
    w0o.start()
    w0p.middle()
    w0o.middle()
    w0p.near_got(0, 3)
    project(x_group, normed0_ref, w0_ref, proj0_ref, True)
    w0p.last()
    w0p.fifth()
    w0o.last()
    w0p.near_got(1, 5)
    project(lax.rem(x_group + 3, 4), normed0_ref, w0_ref, proj0_ref, False)
    w0p.near_got(2, 6)
    project(lax.rem(x_group + 1, 4), normed0_ref, w0_ref, proj0_ref, False)
    w0p.end()
    w0p.near_got(4, 7)
    w1[0].start()
    project(lax.rem(x_group + 2, 4), normed0_ref, w0_ref, proj0_ref, False)
    attend(proj0_ref, qkg0, att0_ref, False)
    w0o.fifth()
    w0o.end()
    w0o.near_got(*shards)

    r0 = parted(reduce_of, by_positions, 0, 0)
    for piece, cols in zip(r0.parts, halves):
        branch(att0_ref, w0_ref, part_ref, cols)
        piece.start()
    w1[0].middle()
    w1[1].start()
    r0.middle()
    w1[0].last()
    r0.last()
    swaps = []
    for i, cols in enumerate(halves):
        r0.parts[i].end()
        branch_end(x_ref, positions, gate0, r0.parts[i], own_ref.at[0], 0, cols)
        swaps.append(
            Swap(own_ref.at[0], middle_ref, cols, swap_out(), frames, swap_sems.at[i], local.at[5, i])
        )
        swaps[i].start()
        if i == 0:
            w1[1].middle()
    a0 = parted(gather_of, middle_ref, by_frames, 0)
    for i in range(2):
        swaps[i].wait()
        a0.parts[i].start()
    w1[1].last()
    w1[2].start()
    w1[0].fifth()
    w1[0].end()
    a0.middle()
    w1[2].middle()
    w1[1].fifth()
    w1[1].end()
    a0.last()
    w1[0].near_got(*shards)
    dy_load.wait()
    attended_grad(dy_ref, w1_ref, gate1, datt_ref, whole_rows)
    w1[2].last()
    w1[2].fifth()
    w1[2].end()
    for weights in (w0p, w0o, *w1):
        weights.sent()
    for weights in w1[1:]:
        weights.near_got(*shards)

    proj1_ref[...] = jnp.zeros_like(proj1_ref)
    squares = jnp.zeros((T, 1), F32)
    for piece, cols in zip(a0.parts, halves):
        piece.fifth()
        piece.end()
        squares = project_scaled(middle_ref, w1_ref, gain1, proj1_ref, cols, squares)
    proj1_ref[...] *= lax.rsqrt(squares / D + EPS)
    attend(proj1_ref, qkg1, att1_ref, True)
    branch(att1_ref, w1_ref, part1_ref, whole_rows)
    r1 = Reduce(part1_ref, by_frames, OWN, whole_rows, held_ref.at[1], rs_sems.at[4])
    r1.start()
    grad_cols = ((PC, WC - PC), (0, 384), (384, 384))
    grads1 = [
        WeightGrads(g_ref, cols, far1_ref, g_sems.at[i], near1_ref, gn_sems.at[i]) for i, cols in enumerate(grad_cols)
    ]
    projected_grad(qkg1, proj1_ref, datt_ref, dproj_ref, True)

    r2 = parted(reduce_of, by_frames, 2, 5)
    for piece, cols in zip(r2.parts, halves):
        normed_grad(dproj_ref, w1_ref, part_ref, cols)
        piece.start()
    outw_grads(dy_ref, gate1, att1_ref, g_ref, whole_rows)
    grads1[0].pair()
    normalise(middle_ref, gain1, normed1_ref)
    proj_grads(normed1_ref, dproj_ref, g_ref, grad_cols[1])
    grads1[1].pair()
    grads1[0].start()
    r2.middle()
    proj_grads(normed1_ref, dproj_ref, g_ref, grad_cols[2])
    grads1[2].pair()
    grads1[1].start()
    r2.last()
    grads1[0].middle()
    a0.sent()
    r2.end()
    input_grad(middle_ref, frames, dy_ref, frames, gain1, r2.parts[0], sum_ref, own_ref.at[1], 0)
    a1 = parted(gather_of, grad_ref, by_positions, 4)
    swaps = [
        Swap(own_ref.at[1], grad_ref, cols, swap_back(), positions, swap_sems.at[4 + i], local.at[5, i])
        for i, cols in enumerate(halves)
    ]
    for i in range(2):
        swaps[i].start()
    r1.middle()
    grads1[0].last()
    r1.last()
    for i in range(2):
        swaps[i].wait()
        a1.parts[i].start()
    grads1[1].middle()
    a1.middle()
    r1.end()
    branch_end(middle_ref, frames, gate1, r1, mixed_ref, frames, whole_rows)
    grads1[2].start()
    a1.last()
    a2 = Gather(mixed_ref, by_frames, OWN, whole_rows, ag_sems.at[8])
    a2.start()
    grads1[1].last()
    grads1[2].middle()

    for piece, cols in zip(a1.parts, halves):
        piece.fifth()
        piece.end()
        attended_grad(grad_ref, w0_ref, gate0, datt_ref, cols)
    projected_grad(qkg0, proj0_ref, datt_ref, dproj_ref, False)
    r3 = parted(reduce_of, by_positions, 3, 9)
    for piece, cols in zip(r3.parts, halves):
        normed_grad(dproj_ref, w0_ref, part_ref, cols)
        piece.start()
    near0_ref, far0_ref = w1_ref.at[pl.ds(0, 8 * SH)], w1_ref.at[pl.ds(8 * SH, 7 * SH)]
    grads0 = [
        WeightGrads(w0_ref, cols, far0_ref, g_sems.at[3 + i], near0_ref, gn_sems.at[3 + i])
        for i, cols in enumerate(grad_cols)
    ]
    proj_grads(normed0_ref, dproj_ref, w0_ref, grad_cols[1])
    grads0[1].pair()
    a2.middle()
    proj_grads(normed0_ref, dproj_ref, w0_ref, grad_cols[2])
    grads0[2].pair()
    grads0[1].start()
    r3.middle()
    outw_grads(grad_ref, gate0, att0_ref, w0_ref, whole_rows)
    grads0[0].pair()
    grads0[2].start()
    r3.last()
    grads1[2].last()
    grads0[1].middle()
    grads0[0].start()
    r3.end()
    input_grad(x_ref, positions, grad_ref, positions, gain0, r3.parts[0], sum_ref, clip_ref, positions)
    a3 = parted(gather_of, clip_ref, by_positions, 9, False)
    a3.start()
    a2.last()
    grads0[2].middle()
    a3.middle()
    grads0[1].last()
    grads0[0].middle()
    a3.last()
    grads0[2].last()
    for i in range(3):
        grads1[i].end()
        grads1[i].result(1, gproj_ref, goutw_ref)
    grads0[0].last()
    a1.sent()
    a2.fifth()
    a2.end()
    a2.sent()
    a3.fifth()
    for i in (1, 2, 0):
        grads0[i].end()
        grads0[i].result(0, gproj_ref, goutw_ref)
    a3.end()
    a3.sent()


def shaped(shape, dtype=BF16):
    return jax.ShapeDtypeStruct(shape, dtype)


def sem(*shape):
    return pltpu.SemaphoreType.DMA(shape)


def local_program(clip_tokens, out_cotangent, proj_weight, out_weight, norm_gain, branch_gate, qk_gain):
    in_vmem = pl.BlockSpec(memory_space=pltpu.VMEM)
    anywhere = pl.BlockSpec(memory_space=pl.ANY)
    out_shapes = [(T, D), (T, D), (2, SH, PC), (2, SH, WC - PC)]
    tokens = lambda *lead: pltpu.VMEM((*lead, T, D), BF16)
    mixed, clip, gproj, goutw = pl.pallas_call(
        whole,
        out_shape=[pltpu.VMEM(shape, BF16) for shape in out_shapes],
        in_specs=[anywhere] * 4 + [in_vmem] * 3,
        out_specs=[in_vmem] * 4,
        scratch_shapes=[
            tokens(),
            tokens(),
            pltpu.VMEM((D, WC), BF16),
            pltpu.VMEM((D, WC), BF16),
            pltpu.VMEM((D, WC), BF16),
            tokens(),
            tokens(),
            pltpu.VMEM((T, PC), F32),
            pltpu.VMEM((T, PC), F32),
            pltpu.VMEM((T, 2 * HD), BF16),
            pltpu.VMEM((T, 2 * HD), BF16),
            pltpu.VMEM((T, 2 * HD), F32),
            pltpu.VMEM((T, PC), BF16),
            tokens(),
            tokens(),
            tokens(),
            tokens(),
            pltpu.VMEM((4, 7 * OWN, D), BF16),
            pltpu.VMEM((4, OWN, D), BF16),
            pltpu.VMEM((OWN, D), F32),
            pltpu.VMEM((8 * SH, WC), BF16),
            pltpu.VMEM((7 * SH, WC), BF16),
            sem(5, 2, 9),
            sem(5, 2, 8),
            sem(7, 4),
            sem(13, 2, 9),
            sem(13, 2, 9),
            sem(6, 2, 9),
            sem(6, 2, 8),
            sem(8, 2, 2),
        ],
        compiler_params=pltpu.CompilerParams(
            vmem_limit_bytes=VMEM_LIMIT, collective_id=0, has_side_effects=True
        ),
        name="two_blocks",
    )(
        clip_tokens.reshape(T, D),
        out_cotangent.reshape(T, D),
        proj_weight,
        jnp.swapaxes(out_weight, 1, 2),
        norm_gain,
        branch_gate,
        qk_gain,
    )
    return mixed.reshape(16, 16, D), clip.reshape(1, T, D), gproj, jnp.swapaxes(goutw, 1, 2)


def solution(mesh):
    placed = (
        P("seq", None, None),
        P(None, "seq", None),
        P(None, "seq", "fsdp"),
        P(None, "fsdp", "seq"),
        P(),
        P(),
        P(),
    )
    return jax.shard_map(
        local_program,
        mesh=mesh,
        in_specs=placed,
        out_specs=(
            P(None, "seq", None),
            P("seq", None, None),
            P(None, "seq", "fsdp"),
            P(None, "fsdp", "seq"),
        ),
        check_vma=False,
    )
```
